128 devices in a mesh: expert: 32 (over z, x, y_lo), dp: 4 (over y_hi, core).
Axes of the slice: x: 4, y: 4 (y_hi: 2, y_lo: 2; y = y_hi * 2 + y_lo), z: 4, core: 2. Of those that a mesh axis runs over, the one named last changes fastest.
Arguments:
- tokens: bfloat16 [4096, 5120], P('expert', 'dp'), may hold values from -6 to 6
- cotangent: bfloat16 [4096, 5120], P('expert', 'dp'), may hold values from -6 to 6
- expert_ids: int32 [4096, 6], P('expert'), may hold values from 0 to 159, all different within a row
- route_probs: float32 [4096, 6], P('expert'), may hold values from 0.1 to 1
- w_gate: bfloat16 [32, 5120, 1536], P('expert', None, 'dp'), may hold values from -0.078125 to 0.078125
- w_up: bfloat16 [32, 5120, 1536], P('expert', None, 'dp'), may hold values from -0.078125 to 0.078125
- w_down: bfloat16 [32, 1536, 5120], P('expert', 'dp'), may hold values from -0.15625 to 0.15625
Outputs:
- mixed: bfloat16 [4096, 5120], P('expert', 'dp')
- grad_tokens: bfloat16 [4096, 5120], P('expert', 'dp')
- grad_probs: float32 [4096, 6], P('expert')
- grad_gate: bfloat16 [32, 5120, 1536], P('expert', None, 'dp')
- grad_up: bfloat16 [32, 5120, 1536], P('expert', None, 'dp')
- grad_down: bfloat16 [32, 1536, 5120], P('expert', 'dp')
The draws below stay inside these ranges and needn't reach their ends.
All inputs are finite; a program needn't handle non-finite values.
Results may differ from the reference program's by a relative error of at most 0.0058.
Values may be sent and summed in bfloat16 or wider, within the bound.
No kernel may reach another device: no remote copies, remote signals or barrier semaphores. Data moves between devices by JAX's collectives and lax.ppermute only.
A program may use at most 192 MiB of HBM per device.

```python
import jax
import jax.numpy as jnp
from jax import lax

D = 5120
FF = 1536
ROUTED = 160
TOPK = 6
TOK_DEV = 128
CAP = 12
EXPERTS = 32
TOKENS = 4096
N_EXPERT = 32


def steps_of(own_key, extent, pieces, smallest, top_value):
    def one(position, shards_of):
        steps = jax.random.uniform(jax.random.fold_in(jax.random.fold_in(own_key, 6), position), (shards_of,), jnp.float32, smallest / len(pieces), top_value / len(pieces))
        return jnp.repeat(jnp.exp(steps), extent[position] // shards_of).reshape((-1,) + (1,) * (len(extent) - position - 1))

    gain = one(*pieces[0])
    for cut in pieces[1:]:
        gain = gain * one(*cut)
    return gain


def choose_distinct(stream_key, rows, number_of, top, lift):
    sequence = jax.random.permutation(jax.random.fold_in(stream_key, 1), number_of)
    pull = sequence
    for power in range(3):
        pull = pull * pull // number_of
    pull = pull * lift // number_of
    chance = jax.random.randint(jax.random.fold_in(stream_key, 2), (rows, number_of), 0, 4096) + pull
    holders = jax.random.permutation(jax.random.fold_in(stream_key, 3), rows)[jnp.arange(number_of) % rows]
    chance = jnp.where(jnp.arange(rows)[:, None] == holders[None, :], 1 << 14, chance)
    priority = chance * number_of + jnp.arange(number_of)
    return lax.top_k(priority.astype(jnp.int32), top)[1].astype(jnp.int32)


def bell_draw(key, dims, scale, bound, split=(), held_as=jnp.bfloat16):
    values = scale * jax.random.normal(key, dims, jnp.float32)
    if split:
        values = values * steps_of(key, dims, split, -0.22, 0.18)
    return jnp.clip(values, -bound, bound).astype(held_as)


def setup_inputs(seed: int = 0) -> dict:
    key_of = jax.random.split(jax.random.key(seed), 8)
    return {
        "tokens": bell_draw(key_of[0], (TOKENS, D), 1.0, 6.0, ((0, 32), (1, 4))),
        "cotangent": bell_draw(key_of[1], (TOKENS, D), 1.0, 6.0, ((0, 32), (1, 4))),
        "expert_ids": choose_distinct(key_of[2], TOKENS, ROUTED, TOPK, 614),
        "route_probs": jnp.clip(0.1 + 0.9 * jax.random.uniform(key_of[3], (TOKENS, TOPK), jnp.float32) ** steps_of(key_of[3], (TOKENS, TOPK), ((0, 32),), -0.2, 0.2), 0.1, 1.0),
        "w_gate": bell_draw(key_of[4], (EXPERTS, D, FF), D ** -0.5, 0.078125, ((0, 32), (2, 4))),
        "w_up": bell_draw(key_of[5], (EXPERTS, D, FF), D ** -0.5, 0.078125, ((0, 32), (2, 4))),
        "w_down": bell_draw(key_of[6], (EXPERTS, FF, D), FF ** -0.5, 0.15625, ((0, 32), (1, 4))),
    }


def expert_pass(rows_in, rows_grad, gate_w, up_w, down_w):
    gate_pre = jnp.dot(rows_in, gate_w, preferred_element_type=jnp.float32)
    up_proj = jnp.dot(rows_in, up_w, preferred_element_type=jnp.float32)
    sigma = jax.nn.sigmoid(gate_pre)
    active = gate_pre * sigma
    hidden = (active * up_proj).astype(jnp.bfloat16)
    result = jnp.dot(hidden, down_w, preferred_element_type=jnp.float32)
    d_hidden = lax.dot_general(rows_grad, down_w, (((1,), (1,)), ((), ())), preferred_element_type=jnp.float32)
    d_gate = (d_hidden * up_proj * sigma * (1.0 + gate_pre * (1.0 - sigma))).astype(jnp.bfloat16)
    d_up = (d_hidden * active).astype(jnp.bfloat16)
    g_down = lax.dot_general(hidden, rows_grad, (((0,), (0,)), ((), ())), preferred_element_type=jnp.float32).astype(jnp.bfloat16)
    g_gate = lax.dot_general(rows_in, d_gate, (((0,), (0,)), ((), ())), preferred_element_type=jnp.float32).astype(jnp.bfloat16)
    g_up = lax.dot_general(rows_in, d_up, (((0,), (0,)), ((), ())), preferred_element_type=jnp.float32).astype(jnp.bfloat16)
    backward = lax.dot_general(d_gate, gate_w, (((1,), (1,)), ((), ())), preferred_element_type=jnp.float32)
    backward = backward + lax.dot_general(d_up, up_w, (((1,), (1,)), ((), ())), preferred_element_type=jnp.float32)
    return result, backward, g_gate, g_up, g_down


def reference(tokens, cotangent, expert_ids, route_probs, w_gate, w_up, w_down):
    per_block = TOK_DEV * TOPK
    entries = TOKENS * TOPK
    flat = expert_ids.reshape(-1).astype(jnp.int32)
    blocked = flat.reshape(N_EXPERT, per_block)
    onehot = (blocked[:, :, None] == jnp.arange(EXPERTS, dtype=jnp.int32)[None, None, :]).astype(jnp.int32)
    before = jnp.cumsum(onehot, axis=1) - onehot
    place = jnp.sum(onehot * before, axis=2).reshape(-1).astype(jnp.int32)
    live = (flat < EXPERTS) & (place < CAP)
    source = (jnp.arange(entries, dtype=jnp.int32) // per_block).astype(jnp.int32)
    rows_each = N_EXPERT * CAP
    empty_slot = EXPERTS * rows_each
    target = jnp.where(live, flat * rows_each + source * CAP + place, empty_slot).astype(jnp.int32)
    slot_entry = jnp.full((empty_slot + 1,), entries, jnp.int32).at[target].set(jnp.arange(entries, dtype=jnp.int32))
    slot_entry = slot_entry[:-1].reshape(EXPERTS, rows_each)
    tok_pad = jnp.concatenate([tokens, jnp.zeros((1, D), jnp.bfloat16)], axis=0)
    cot_pad = jnp.concatenate([cotangent, jnp.zeros((1, D), jnp.bfloat16)], axis=0)
    prob_pad = jnp.concatenate([route_probs.reshape(-1), jnp.zeros((1,), jnp.float32)], axis=0)

    def one_expert(packed):
        entry, gate_w, up_w, down_w = packed
        token_of = (entry // TOPK).astype(jnp.int32)
        rows_in = tok_pad[token_of]
        rows_grad = (prob_pad[entry][:, None] * cot_pad[token_of].astype(jnp.float32)).astype(jnp.bfloat16)
        return expert_pass(rows_in, rows_grad, gate_w, up_w, down_w)

    results, backs, g_gate, g_up, g_down = lax.map(one_expert, (slot_entry, w_gate, w_up, w_down))
    slot_of = jnp.where(live, target, empty_slot).astype(jnp.int32)
    result_pad = jnp.concatenate([results.reshape(-1, D), jnp.zeros((1, D), jnp.float32)], axis=0)
    result_tk = result_pad[slot_of].reshape(TOKENS, TOPK, D)
    mixed = jnp.sum(route_probs[:, :, None] * result_tk, axis=1).astype(jnp.bfloat16)
    grad_probs = jnp.sum(cotangent.astype(jnp.float32)[:, None, :] * result_tk, axis=2)
    back_pad = jnp.concatenate([backs.reshape(-1, D), jnp.zeros((1, D), jnp.float32)], axis=0)
    grad_tokens = jnp.sum(back_pad[slot_of].reshape(TOKENS, TOPK, D), axis=1).astype(jnp.bfloat16)
    return mixed, grad_tokens, grad_probs, g_gate, g_up, g_down
```

```python
import functools

import jax
import jax.numpy as jnp
from jax import lax
from jax.experimental import pallas as pl
from jax.experimental.pallas import tpu as pltpu
from jax.sharding import Mesh, PartitionSpec as P

BF = jnp.bfloat16
F32 = jnp.float32

EXPERTS = 32
BLOCK = 128
TOPK = 6
COLS = 1280
HALF = 640
HID = 384
ROWS = 384
MAIN = 256
REST = 128
WIDE = COLS + HALF
D = 4 * COLS
VMEM = 40 * 1024 * 1024


def _dot(a, b):
    return jnp.dot(a, b, preferred_element_type=F32)


def _dot_nt(a, b):
    return lax.dot_general(a, b, (((1,), (1,)), ((), ())), preferred_element_type=F32)


def _dot_tn(a, b):
    return lax.dot_general(a, b, (((0,), (0,)), ((), ())), preferred_element_type=F32)


def _iota(shape, dim):
    return lax.broadcasted_iota(jnp.int32, shape, dim)


def _routing(ids_t, probs_t):
    expert = _iota((EXPERTS, BLOCK), 0)
    chosen = jnp.zeros((EXPERTS, BLOCK), F32)
    weight = jnp.zeros((EXPERTS, BLOCK), F32)
    for k in range(TOPK):
        hit = ids_t[k : k + 1, :] == expert
        chosen = jnp.where(hit, 1.0, chosen)
        weight = jnp.where(hit, probs_t[k : k + 1, :], weight)
    earlier = (_iota((BLOCK, BLOCK), 0) < _iota((BLOCK, BLOCK), 1)).astype(F32).astype(BF)
    before = _dot(chosen.astype(BF), earlier)
    code = jnp.where(chosen > 0.5, before, -1.0)
    row = _iota((MAIN, EXPERTS), 0)
    spread = ((row // 8) == _iota((MAIN, EXPERTS), 1)).astype(F32).astype(BF)
    place = _dot(spread, code.astype(BF))
    j = _iota((MAIN, BLOCK), 0)
    main = jnp.where(place == (j % 8).astype(F32), 1.0, 0.0)
    rest = jnp.where(place == (8 + j % 4).astype(F32), 1.0, 0.0)
    hi = weight.astype(BF)
    left = weight - hi.astype(F32)
    mid = left.astype(BF)
    low = (left - mid.astype(F32)).astype(BF)
    full = _dot(spread, hi) + _dot(spread, mid) + _dot(spread, low)
    return main, rest, full


def _lower_half(shape):
    return (_iota(shape, 0) % 8) < 4


def _send(main, rest, source):
    first = _lower_half((MAIN, BLOCK))
    p0 = jnp.where(first, rest, 0.0).astype(BF)
    p1 = jnp.where(first, 0.0, rest).astype(BF)
    a = _dot(main.astype(BF), source)
    b = _dot(p0, source[:, :HALF]) + _dot(p1, source[:, HALF:])
    return a, b


def _pack_rows_kernel(ids_ref, probs_ref, tok_ref, out_ref):
    main, rest, _ = _routing(ids_ref[...], probs_ref[...])
    a, b = _send(main, rest, tok_ref[...])
    a, b = a.astype(BF), b.astype(BF)
    for y in range(2):
        out_ref[y, :, :COLS] = a
        out_ref[y, :, COLS:] = b


def _pack_grads_kernel(ids_ref, probs_ref, cot_ref, out_ref, pick_ref, weight_ref):
    main, rest, full = _routing(ids_ref[...], probs_ref[...])
    a, b = _send(main, rest, cot_ref[...])
    wm, wr = main * full, rest * full
    a = (a * jnp.sum(wm, axis=1, keepdims=True)).astype(BF)
    b = (b * jnp.sum(wr, axis=1, keepdims=True)).astype(BF)
    for y in range(2):
        out_ref[y, :, :COLS] = a
        out_ref[y, :, COLS:] = b
    pick_ref[:MAIN, :] = main.astype(BF)
    pick_ref[MAIN:, :] = rest.astype(BF)
    weight_ref[:MAIN, :] = wm
    weight_ref[MAIN:, :] = wr


def _fold(h):
    q = _iota((REST, MAIN), 0)
    return (_iota((REST, MAIN), 1) == (q // 4) * 8 + 4 * h + q % 4).astype(F32).astype(BF)


def _fold_t(h):
    q = _iota((MAIN, REST), 1)
    return (_iota((MAIN, REST), 0) == (q // 4) * 8 + 4 * h + q % 4).astype(F32).astype(BF)


def _unpack(r_ref, x_ref):
    rest = r_ref[0, :, COLS:]
    x_ref[:MAIN, :] = r_ref[0, :, :COLS]
    x_ref[MAIN:, :HALF] = _dot(_fold(0), rest).astype(BF)
    x_ref[MAIN:, HALF:] = _dot(_fold(1), rest).astype(BF)


def _pack(value, out_ref):
    rest = value[MAIN:, :]
    out_ref[0, :, :COLS] = value[:MAIN, :]
    out_ref[0, :, COLS:] = (_dot(_fold_t(0), rest[:, :HALF]) + _dot(_fold_t(1), rest[:, HALF:])).astype(BF)


def _forward_kernel(core_ref, own_ref, other_ref, wg_ref, wu_ref, x_ref, g_ref, u_ref, h_ref):
    step = pl.program_id(0)

    @pl.when(step < 2)
    def _():
        _unpack(own_ref, x_ref)

    @pl.when(step >= 2)
    def _():
        _unpack(other_ref, x_ref)

    x = x_ref[...]
    g = _dot(x, wg_ref[...])
    u = _dot(x, wu_ref[...])

    @pl.when(step == 0)
    def _():
        g_ref[...] = g
        u_ref[...] = u

    @pl.when(step > 0)
    def _():
        g_ref[...] += g
        u_ref[...] += u

    @pl.when(step == 3)
    def _():
        gate = g_ref[...]
        h_ref[...] = (gate * jax.nn.sigmoid(gate) * u_ref[...]).astype(BF)


def _backward_kernel(core_ref, own_ref, other_ref, wd_ref, g_ref, u_ref, e_ref, d_ref, a_ref):
    step = pl.program_id(0)

    @pl.when(step < 2)
    def _():
        _unpack(own_ref, e_ref)

    @pl.when(step >= 2)
    def _():
        _unpack(other_ref, e_ref)

    a = _dot_nt(e_ref[...], wd_ref[...])

    @pl.when(step == 0)
    def _():
        a_ref[...] = a

    @pl.when(step > 0)
    def _():
        a_ref[...] += a

    @pl.when(step == 3)
    def _():
        total, gate = a_ref[...], g_ref[...]
        s = jax.nn.sigmoid(gate)
        d_ref[:, :HID] = (total * u_ref[...] * s * (1.0 + gate * (1.0 - s))).astype(BF)
        d_ref[:, HID:] = (total * (gate * s)).astype(BF)


def _result_kernel(core_ref, h_ref, hp_ref, wd_ref, wdp_ref, out_ref):
    value = _dot(h_ref[...], wd_ref[...]) + _dot(hp_ref[...], wdp_ref[...])
    _pack(value.astype(BF), out_ref)


def _back_kernel(core_ref, d_ref, dp_ref, wg_ref, wu_ref, wgp_ref, wup_ref, out_ref):
    value = _dot_nt(d_ref[:, :HID], wg_ref[...]) + _dot_nt(d_ref[:, HID:], wu_ref[...])
    value += _dot_nt(dp_ref[:, :HID], wgp_ref[...]) + _dot_nt(dp_ref[:, HID:], wup_ref[...])
    _pack(value.astype(BF), out_ref)


def _home(pick, r_ref):
    main = pick[:MAIN, :]
    first = _lower_half((MAIN, BLOCK))
    rest = pick[MAIN:, :].astype(F32)
    halves = (jnp.where(first, rest, 0.0).astype(BF), jnp.where(first, 0.0, rest).astype(BF))
    out = []
    for h in range(2):
        total = jnp.zeros((BLOCK, HALF), F32)
        for y in range(2):
            total += _dot_tn(main, r_ref[y, :, h * HALF : (h + 1) * HALF])
            total += _dot_tn(halves[h], r_ref[y, :, COLS:])
        out.append(total)
    return out


def _mixed_kernel(ids_ref, pick_ref, weight_ref, cot_ref, r_ref, mixed_ref, gp_ref):
    w = weight_ref[...]
    hi = w.astype(BF)
    lo = (w - hi.astype(F32)).astype(BF)
    top, bottom = _home(hi, r_ref), _home(lo, r_ref)
    for h in range(2):
        mixed_ref[:, h * HALF : (h + 1) * HALF] = (top[h] + bottom[h]).astype(BF)
    cot = cot_ref[...]
    first = _lower_half((MAIN, BLOCK))
    inner = jnp.zeros((MAIN, BLOCK), F32)
    inner_rest = jnp.zeros((MAIN, BLOCK), F32)
    for y in range(2):
        inner += _dot_nt(r_ref[y, :, :COLS], cot)
        rest = r_ref[y, :, COLS:]
        inner_rest += jnp.where(first, _dot_nt(rest, cot[:, :HALF]), _dot_nt(rest, cot[:, HALF:]))
    pick = pick_ref[...].astype(F32)
    both = pick[:MAIN, :] * inner + pick[MAIN:, :] * inner_rest
    each = jnp.sum(both.reshape(EXPERTS, 8, BLOCK), axis=1)
    expert = _iota((EXPERTS, BLOCK), 0)
    ids = ids_ref[...]
    for k in range(TOPK):
        gp_ref[k : k + 1, :] = jnp.sum(jnp.where(ids[k : k + 1, :] == expert, each, 0.0), axis=0, keepdims=True)
    gp_ref[TOPK:, :] = jnp.zeros((8 - TOPK, BLOCK), F32)


def _grad_tokens_kernel(pick_ref, r_ref, out_ref):
    halves = _home(pick_ref[...], r_ref)
    for h in range(2):
        out_ref[:, h * HALF : (h + 1) * HALF] = halves[h].astype(BF)


def _params():
    return pltpu.CompilerParams(vmem_limit_bytes=VMEM)


def _cost(flops, moved):
    return pl.CostEstimate(flops=int(flops), bytes_accessed=int(moved), transcendentals=0)


def _shape(shape, dtype):
    return jax.ShapeDtypeStruct(shape, dtype)


def _src(step):
    return step // 2


def _group(step, core):
    return (step % 2) * 2 + jnp.where(step < 2, core, 1 - core)


def _received():
    own = pl.BlockSpec((1, MAIN, WIDE), lambda i, c: (jnp.minimum(i, 1), 0, 0))
    other = pl.BlockSpec((1, MAIN, WIDE), lambda i, c: (jnp.maximum(i - 2, 0), 0, 0))
    return own, other


def _fixed(*shape):
    return pl.BlockSpec(shape, lambda i, c: (0,) * len(shape))


def _forward(core, own, other, w_gate, w_up):
    weight = pl.BlockSpec((COLS, HID), lambda i, c: (_group(i, c[0]), 0))
    return pl.pallas_call(
        _forward_kernel,
        grid_spec=pltpu.PrefetchScalarGridSpec(
            num_scalar_prefetch=1,
            grid=(4,),
            in_specs=[*_received(), weight, weight],
            out_specs=[
                pl.BlockSpec((ROWS, COLS), lambda i, c: (0, _group(i, c[0]))),
                _fixed(ROWS, HID),
                _fixed(ROWS, HID),
                _fixed(ROWS, HID),
            ],
        ),
        out_shape=[
            _shape((ROWS, D), BF),
            _shape((ROWS, HID), F32),
            _shape((ROWS, HID), F32),
            _shape((ROWS, HID), BF),
        ],
        compiler_params=_params(),
        cost_estimate=_cost(4 * ROWS * D * HID, 17e6),
        name="forward",
    )(core, own, other, w_gate, w_up)


def _backward(core, own, other, w_down, gate, up):
    return pl.pallas_call(
        _backward_kernel,
        grid_spec=pltpu.PrefetchScalarGridSpec(
            num_scalar_prefetch=1,
            grid=(4,),
            in_specs=[
                *_received(),
                pl.BlockSpec((HID, COLS), lambda i, c: (0, _group(i, c[0]))),
                _fixed(ROWS, HID),
                _fixed(ROWS, HID),
            ],
            out_specs=[
                pl.BlockSpec((ROWS, COLS), lambda i, c: (0, _group(i, c[0]))),
                _fixed(ROWS, 2 * HID),
            ],
            scratch_shapes=[pltpu.VMEM((ROWS, HID), F32)],
        ),
        out_shape=[_shape((ROWS, D), BF), _shape((ROWS, 2 * HID), BF)],
        compiler_params=_params(),
        cost_estimate=_cost(2 * ROWS * D * HID, 14e6),
        name="backward",
    )(core, own, other, w_down, gate, up)


def _result(core, hidden, hidden_p, w_down, w_down_p):
    weight = pl.BlockSpec((HID, COLS), lambda i, c: (0, 2 * i + c[0]))
    return pl.pallas_call(
        _result_kernel,
        grid_spec=pltpu.PrefetchScalarGridSpec(
            num_scalar_prefetch=1,
            grid=(2,),
            in_specs=[_fixed(ROWS, HID), _fixed(ROWS, HID), weight, weight],
            out_specs=pl.BlockSpec((1, MAIN, WIDE), lambda i, c: (i, 0, 0)),
        ),
        out_shape=_shape((2, MAIN, WIDE), BF),
        compiler_params=_params(),
        cost_estimate=_cost(2 * ROWS * D * HID, 7e6),
        name="result",
    )(core, hidden, hidden_p, w_down, w_down_p)


def _back(core, grads, grads_p, w_gate, w_up, w_gate_p, w_up_p):
    weight = pl.BlockSpec((COLS, HID), lambda i, c: (2 * i + c[0], 0))
    return pl.pallas_call(
        _back_kernel,
        grid_spec=pltpu.PrefetchScalarGridSpec(
            num_scalar_prefetch=1,
            grid=(2,),
            in_specs=[_fixed(ROWS, 2 * HID), _fixed(ROWS, 2 * HID), weight, weight, weight, weight],
            out_specs=pl.BlockSpec((1, MAIN, WIDE), lambda i, c: (i, 0, 0)),
        ),
        out_shape=_shape((2, MAIN, WIDE), BF),
        compiler_params=_params(),
        cost_estimate=_cost(4 * ROWS * D * HID, 11e6),
        name="back",
    )(core, grads, grads_p, w_gate, w_up, w_gate_p, w_up_p)


def _local(kernel, out_shape, flops, moved, name, *args):
    return pl.pallas_call(
        kernel, out_shape=out_shape, compiler_params=_params(), cost_estimate=_cost(flops, moved), name=name
    )(*args)


def _exchange(packed):
    chunks = packed.reshape(2 * EXPERTS, 8, WIDE)
    got = lax.all_to_all(chunks, ("yhi", "expert"), split_axis=0, concat_axis=0, tiled=True)
    return got.reshape(2, MAIN, WIDE)


def _swap(value, axis="core"):
    return lax.ppermute(value, axis, [(0, 1), (1, 0)])


def body(tokens, cotangent, expert_ids, route_probs, w_gate, w_up, w_down):
    core = lax.axis_index("core").astype(jnp.int32).reshape(1)
    wg, wu, wd = w_gate[0], w_up[0], w_down[0]
    ids_t, probs_t = expert_ids.T, route_probs.T

    send_x = _local(_pack_rows_kernel, _shape((2, MAIN, WIDE), BF), 2e8, 3e6, "pack_rows", ids_t, probs_t, tokens)
    recv_x = _exchange(send_x)
    send_e, pick, weight = _local(
        _pack_grads_kernel,
        [_shape((2, MAIN, WIDE), BF), _shape((2 * MAIN, BLOCK), BF), _shape((2 * MAIN, BLOCK), F32)],
        2e8,
        3e6,
        "pack_grads",
        ids_t,
        probs_t,
        cotangent,
    )
    wd_p, wg_p, wu_p = _swap(wd), _swap(wg), _swap(wu)
    recv_e = _exchange(send_e)

    x, gate, up, hidden = _forward(core, recv_x, _swap(recv_x), wg, wu)
    send_o = _result(core, hidden, _swap(hidden), wd, wd_p)
    recv_o = _exchange(send_o)

    e, grads = _backward(core, recv_e, _swap(recv_e), wd, gate, up)
    send_b = _back(core, grads, _swap(grads), wg, wu, wg_p, wu_p)
    recv_b = _exchange(send_b)

    g_down = _dot_tn(hidden, e).astype(BF)
    g_gate = _dot_tn(x, grads[:, :HID]).astype(BF)
    g_up = _dot_tn(x, grads[:, HID:]).astype(BF)

    mixed, inner = _local(
        _mixed_kernel,
        [_shape((BLOCK, COLS), BF), _shape((8, BLOCK), F32)],
        4e8,
        3e6,
        "mixed",
        ids_t,
        pick,
        weight,
        cotangent,
        recv_o,
    )
    inner = inner + _swap(inner)
    inner = inner + _swap(inner, "yhi")
    grad_probs = inner[:TOPK].T

    grad_tokens = _local(_grad_tokens_kernel, _shape((BLOCK, COLS), BF), 2e8, 3e6, "grad_tokens", pick, recv_b)
    return mixed, grad_tokens, grad_probs, g_gate[None], g_up[None], g_down[None]


def solution(mesh):
    fine = Mesh(mesh.devices.reshape(EXPERTS, 2, 2), ("expert", "yhi", "core"))
    dp = ("yhi", "core")
    return jax.shard_map(
        body,
        mesh=fine,
        in_specs=(
            P("expert", dp),
            P("expert", dp),
            P("expert", None),
            P("expert", None),
            P("expert", None, dp),
            P("expert", None, dp),
            P("expert", dp, None),
        ),
        out_specs=(
            P("expert", dp),
            P("expert", dp),
            P("expert", None),
            P("expert", None, dp),
            P("expert", None, dp),
            P("expert", dp, None),
        ),
        check_vma=False,
    )
```

```python
import functools

import jax
import jax.numpy as jnp
from jax import lax
from jax.experimental import pallas as pl
from jax.experimental.pallas import tpu as pltpu
from jax.sharding import Mesh, PartitionSpec as P

BF = jnp.bfloat16
F32 = jnp.float32

EXPERTS = 32
BLOCK = 128
TOPK = 6
COLS = 1280
HALF = 640
HID = 384
ROWS = 384
MAIN = 256
REST = 128
WIDE = COLS + HALF
D = 4 * COLS
VMEM = 40 * 1024 * 1024


def _dot(a, b):
    return jnp.dot(a, b, preferred_element_type=F32)


def _dot_nt(a, b):
    return lax.dot_general(a, b, (((1,), (1,)), ((), ())), preferred_element_type=F32)


def _dot_tn(a, b):
    return lax.dot_general(a, b, (((0,), (0,)), ((), ())), preferred_element_type=F32)


def _iota(shape, dim):
    return lax.broadcasted_iota(jnp.int32, shape, dim)


def _routing(ids_t, probs_t):
    expert = _iota((EXPERTS, BLOCK), 0)
    chosen = jnp.zeros((EXPERTS, BLOCK), F32)
    weight = jnp.zeros((EXPERTS, BLOCK), F32)
    for k in range(TOPK):
        hit = ids_t[k : k + 1, :] == expert
        chosen = jnp.where(hit, 1.0, chosen)
        weight = jnp.where(hit, probs_t[k : k + 1, :], weight)
    earlier = (_iota((BLOCK, BLOCK), 0) < _iota((BLOCK, BLOCK), 1)).astype(F32).astype(BF)
    before = _dot(chosen.astype(BF), earlier)
    code = jnp.where(chosen > 0.5, before, -1.0)
    row = _iota((MAIN, EXPERTS), 0)
    spread = ((row // 8) == _iota((MAIN, EXPERTS), 1)).astype(F32).astype(BF)
    place = _dot(spread, code.astype(BF))
    j = _iota((MAIN, BLOCK), 0)
    main = jnp.where(place == (j % 8).astype(F32), 1.0, 0.0)
    rest = jnp.where(place == (8 + j % 4).astype(F32), 1.0, 0.0)
    hi = weight.astype(BF)
    left = weight - hi.astype(F32)
    mid = left.astype(BF)
    low = (left - mid.astype(F32)).astype(BF)
    full = _dot(spread, hi) + _dot(spread, mid) + _dot(spread, low)
    return main, rest, full


def _lower_half(shape):
    return (_iota(shape, 0) % 8) < 4


def _send(main, rest, source):
    first = _lower_half((MAIN, BLOCK))
    p0 = jnp.where(first, rest, 0.0).astype(BF)
    p1 = jnp.where(first, 0.0, rest).astype(BF)
    a = _dot(main.astype(BF), source)
    b = _dot(p0, source[:, :HALF]) + _dot(p1, source[:, HALF:])
    return a, b


def _pack_rows_kernel(ids_ref, probs_ref, tok_ref, out_ref):
    main, rest, _ = _routing(ids_ref[...], probs_ref[...])
    a, b = _send(main, rest, tok_ref[...])
    a, b = a.astype(BF), b.astype(BF)
    for y in range(2):
        out_ref[y, :, :COLS] = a
        out_ref[y, :, COLS:] = b


def _pack_grads_kernel(ids_ref, probs_ref, cot_ref, out_ref, pick_ref, weight_ref):
    main, rest, full = _routing(ids_ref[...], probs_ref[...])
    a, b = _send(main, rest, cot_ref[...])
    wm, wr = main * full, rest * full
    a = (a * jnp.sum(wm, axis=1, keepdims=True)).astype(BF)
    b = (b * jnp.sum(wr, axis=1, keepdims=True)).astype(BF)
    for y in range(2):
        out_ref[y, :, :COLS] = a
        out_ref[y, :, COLS:] = b
    pick_ref[:MAIN, :] = main.astype(BF)
    pick_ref[MAIN:, :] = rest.astype(BF)
    weight_ref[:MAIN, :] = wm
    weight_ref[MAIN:, :] = wr


def _fold(h):
    q = _iota((REST, MAIN), 0)
    return (_iota((REST, MAIN), 1) == (q // 4) * 8 + 4 * h + q % 4).astype(F32).astype(BF)


def _fold_t(h):
    q = _iota((MAIN, REST), 1)
    return (_iota((MAIN, REST), 0) == (q // 4) * 8 + 4 * h + q % 4).astype(F32).astype(BF)


def _unpack(r_ref, x_ref):
    rest = r_ref[0, :, COLS:]
    x_ref[:MAIN, :] = r_ref[0, :, :COLS]
    x_ref[MAIN:, :HALF] = _dot(_fold(0), rest).astype(BF)
    x_ref[MAIN:, HALF:] = _dot(_fold(1), rest).astype(BF)


def _pack(value, out_ref):
    rest = value[MAIN:, :]
    out_ref[0, :, :COLS] = value[:MAIN, :]
    out_ref[0, :, COLS:] = (_dot(_fold_t(0), rest[:, :HALF]) + _dot(_fold_t(1), rest[:, HALF:])).astype(BF)


def _forward_kernel(core_ref, own_ref, other_ref, wg_ref, wu_ref, x_ref, g_ref, u_ref, h_ref):
    step = pl.program_id(0)

    @pl.when(step < 2)
    def _():
        _unpack(own_ref, x_ref)

    @pl.when(step >= 2)
    def _():
        _unpack(other_ref, x_ref)

    x = x_ref[...]
    g = _dot(x, wg_ref[...])
    u = _dot(x, wu_ref[...])

    @pl.when(step == 0)
    def _():
        g_ref[...] = g
        u_ref[...] = u

    @pl.when(step > 0)
    def _():
        g_ref[...] += g
        u_ref[...] += u

    @pl.when(step == 3)
    def _():
        gate = g_ref[...]
        h_ref[...] = (gate * jax.nn.sigmoid(gate) * u_ref[...]).astype(BF)


def _backward_kernel(core_ref, own_ref, other_ref, wd_ref, g_ref, u_ref, e_ref, d_ref, a_ref):
    step = pl.program_id(0)

    @pl.when(step < 2)
    def _():
        _unpack(own_ref, e_ref)

    @pl.when(step >= 2)
    def _():
        _unpack(other_ref, e_ref)

    a = _dot_nt(e_ref[...], wd_ref[...])

    @pl.when(step == 0)
    def _():
        a_ref[...] = a

    @pl.when(step > 0)
    def _():
        a_ref[...] += a

    @pl.when(step == 3)
    def _():
        total, gate = a_ref[...], g_ref[...]
        s = jax.nn.sigmoid(gate)
        d_ref[:, :HID] = (total * u_ref[...] * s * (1.0 + gate * (1.0 - s))).astype(BF)
        d_ref[:, HID:] = (total * (gate * s)).astype(BF)


def _result_kernel(core_ref, h_ref, hp_ref, wd_ref, wdp_ref, out_ref):
    value = _dot(h_ref[...], wd_ref[...]) + _dot(hp_ref[...], wdp_ref[...])
    _pack(value.astype(BF), out_ref)


def _back_kernel(core_ref, d_ref, dp_ref, wg_ref, wu_ref, wgp_ref, wup_ref, out_ref):
    value = _dot_nt(d_ref[:, :HID], wg_ref[...]) + _dot_nt(d_ref[:, HID:], wu_ref[...])
    value += _dot_nt(dp_ref[:, :HID], wgp_ref[...]) + _dot_nt(dp_ref[:, HID:], wup_ref[...])
    _pack(value.astype(BF), out_ref)


def _home(pick, r_ref):
    main = pick[:MAIN, :]
    first = _lower_half((MAIN, BLOCK))
    rest = pick[MAIN:, :].astype(F32)
    halves = (jnp.where(first, rest, 0.0).astype(BF), jnp.where(first, 0.0, rest).astype(BF))
    out = []
    for h in range(2):
        total = jnp.zeros((BLOCK, HALF), F32)
        for y in range(2):
            total += _dot_tn(main, r_ref[y, :, h * HALF : (h + 1) * HALF])
            total += _dot_tn(halves[h], r_ref[y, :, COLS:])
        out.append(total)
    return out


def _mixed_kernel(ids_ref, pick_ref, weight_ref, cot_ref, r_ref, mixed_ref, gp_ref):
    w = weight_ref[...]
    hi = w.astype(BF)
    lo = (w - hi.astype(F32)).astype(BF)
    top, bottom = _home(hi, r_ref), _home(lo, r_ref)
    for h in range(2):
        mixed_ref[:, h * HALF : (h + 1) * HALF] = (top[h] + bottom[h]).astype(BF)
    cot = cot_ref[...]
    first = _lower_half((MAIN, BLOCK))
    inner = jnp.zeros((MAIN, BLOCK), F32)
    inner_rest = jnp.zeros((MAIN, BLOCK), F32)
    for y in range(2):
        inner += _dot_nt(r_ref[y, :, :COLS], cot)
        rest = r_ref[y, :, COLS:]
        inner_rest += jnp.where(first, _dot_nt(rest, cot[:, :HALF]), _dot_nt(rest, cot[:, HALF:]))
    pick = pick_ref[...].astype(F32)
    both = pick[:MAIN, :] * inner + pick[MAIN:, :] * inner_rest
    each = jnp.sum(both.reshape(EXPERTS, 8, BLOCK), axis=1)
    expert = _iota((EXPERTS, BLOCK), 0)
    ids = ids_ref[...]
    for k in range(TOPK):
        gp_ref[k : k + 1, :] = jnp.sum(jnp.where(ids[k : k + 1, :] == expert, each, 0.0), axis=0, keepdims=True)


def _grad_tokens_kernel(pick_ref, r_ref, inner_ref, far_ref, out_ref, gp_ref):
    gp_ref[...] = inner_ref[...] + far_ref[...]
    halves = _home(pick_ref[...], r_ref)
    for h in range(2):
        out_ref[:, h * HALF : (h + 1) * HALF] = halves[h].astype(BF)


def _params():
    return pltpu.CompilerParams(vmem_limit_bytes=VMEM)


def _cost(flops, moved):
    return pl.CostEstimate(flops=int(flops), bytes_accessed=int(moved), transcendentals=0)


def _shape(shape, dtype):
    return jax.ShapeDtypeStruct(shape, dtype)


def _hbm(value):
    return pltpu.with_memory_space_constraint(value, pltpu.HBM)


def _group(step, core):
    return (step % 2) * 2 + jnp.where(step < 2, core, 1 - core)


def _received():
    own = pl.BlockSpec((1, MAIN, WIDE), lambda i, c: (jnp.minimum(i, 1), 0, 0))
    other = pl.BlockSpec((1, MAIN, WIDE), lambda i, c: (jnp.maximum(i - 2, 0), 0, 0))
    return own, other


def _fixed(*shape):
    return pl.BlockSpec(shape, lambda i, c: (0,) * len(shape))


def _forward(core, own, other, w_gate, w_up):
    weight = pl.BlockSpec((COLS, HID), lambda i, c: (_group(i, c[0]), 0))
    return pl.pallas_call(
        _forward_kernel,
        grid_spec=pltpu.PrefetchScalarGridSpec(
            num_scalar_prefetch=1,
            grid=(4,),
            in_specs=[*_received(), weight, weight],
            out_specs=[
                pl.BlockSpec((ROWS, COLS), lambda i, c: (0, _group(i, c[0]))),
                _fixed(ROWS, HID),
                _fixed(ROWS, HID),
                _fixed(ROWS, HID),
            ],
        ),
        out_shape=[
            pltpu.HBM((ROWS, D), BF),
            _shape((ROWS, HID), F32),
            _shape((ROWS, HID), F32),
            _shape((ROWS, HID), BF),
        ],
        compiler_params=_params(),
        cost_estimate=_cost(4 * ROWS * D * HID, 17e6),
        name="forward",
    )(core, _hbm(own), _hbm(other), _hbm(w_gate), _hbm(w_up))


def _backward(core, own, other, w_down, gate, up):
    return pl.pallas_call(
        _backward_kernel,
        grid_spec=pltpu.PrefetchScalarGridSpec(
            num_scalar_prefetch=1,
            grid=(4,),
            in_specs=[
                *_received(),
                pl.BlockSpec((HID, COLS), lambda i, c: (0, _group(i, c[0]))),
                _fixed(ROWS, HID),
                _fixed(ROWS, HID),
            ],
            out_specs=[
                pl.BlockSpec((ROWS, COLS), lambda i, c: (0, _group(i, c[0]))),
                _fixed(ROWS, 2 * HID),
            ],
            scratch_shapes=[pltpu.VMEM((ROWS, HID), F32)],
        ),
        out_shape=[pltpu.HBM((ROWS, D), BF), _shape((ROWS, 2 * HID), BF)],
        compiler_params=_params(),
        cost_estimate=_cost(2 * ROWS * D * HID, 14e6),
        name="backward",
    )(core, _hbm(own), _hbm(other), _hbm(w_down), gate, up)


def _result(core, hidden, hidden_p, w_down, w_down_p):
    weight = pl.BlockSpec((HID, COLS), lambda i, c: (0, 2 * i + c[0]))
    return pl.pallas_call(
        _result_kernel,
        grid_spec=pltpu.PrefetchScalarGridSpec(
            num_scalar_prefetch=1,
            grid=(2,),
            in_specs=[_fixed(ROWS, HID), _fixed(ROWS, HID), weight, weight],
            out_specs=pl.BlockSpec((1, MAIN, WIDE), lambda i, c: (i, 0, 0)),
        ),
        out_shape=pltpu.HBM((2, MAIN, WIDE), BF),
        compiler_params=_params(),
        cost_estimate=_cost(2 * ROWS * D * HID, 7e6),
        name="result",
    )(core, hidden, hidden_p, _hbm(w_down), _hbm(w_down_p))


def _back(core, grads, grads_p, w_gate, w_up, w_gate_p, w_up_p):
    weight = pl.BlockSpec((COLS, HID), lambda i, c: (2 * i + c[0], 0))
    return pl.pallas_call(
        _back_kernel,
        grid_spec=pltpu.PrefetchScalarGridSpec(
            num_scalar_prefetch=1,
            grid=(2,),
            in_specs=[_fixed(ROWS, 2 * HID), _fixed(ROWS, 2 * HID), weight, weight, weight, weight],
            out_specs=pl.BlockSpec((1, MAIN, WIDE), lambda i, c: (i, 0, 0)),
        ),
        out_shape=pltpu.HBM((2, MAIN, WIDE), BF),
        compiler_params=_params(),
        cost_estimate=_cost(4 * ROWS * D * HID, 11e6),
        name="back",
    )(core, grads, grads_p, _hbm(w_gate), _hbm(w_up), _hbm(w_gate_p), _hbm(w_up_p))


def _local(kernel, out_shape, flops, moved, name, *args):
    return pl.pallas_call(
        kernel, out_shape=out_shape, compiler_params=_params(), cost_estimate=_cost(flops, moved), name=name
    )(*args)


def _exchange(packed):
    chunks = packed.reshape(2 * EXPERTS, 8, WIDE)
    got = lax.all_to_all(chunks, ("yhi", "expert"), split_axis=0, concat_axis=0, tiled=True)
    return got.reshape(2, MAIN, WIDE)


def _swap(value, axis="core"):
    return lax.ppermute(value, axis, [(0, 1), (1, 0)])


def body(tokens, cotangent, expert_ids, route_probs, w_gate, w_up, w_down):
    core = lax.axis_index("core").astype(jnp.int32).reshape(1)
    wg, wu, wd = w_gate[0], w_up[0], w_down[0]
    ids_t, probs_t = expert_ids.T, route_probs.T

    send_x = _local(_pack_rows_kernel, pltpu.HBM((2, MAIN, WIDE), BF), 2e8, 3e6, "pack_rows", _hbm(ids_t), _hbm(probs_t), _hbm(tokens))
    recv_x = _exchange(send_x)
    send_e, pick, weight = _local(
        _pack_grads_kernel,
        [pltpu.HBM((2, MAIN, WIDE), BF), _shape((2 * MAIN, BLOCK), BF), _shape((2 * MAIN, BLOCK), F32)],
        2e8,
        3e6,
        "pack_grads",
        _hbm(ids_t),
        _hbm(probs_t),
        _hbm(cotangent),
    )
    wd_p, wg_p, wu_p = _swap(wd), _swap(wg), _swap(wu)
    recv_x, send_e = lax.optimization_barrier((recv_x, send_e))
    recv_e = _exchange(send_e)

    x, gate, up, hidden = _forward(core, recv_x, _swap(recv_x), wg, wu)
    send_o = _result(core, hidden, _swap(hidden), wd, wd_p)
    recv_e, send_o = lax.optimization_barrier((recv_e, send_o))
    recv_o = _exchange(send_o)

    e, grads = _backward(core, recv_e, _swap(recv_e), wd, gate, up)
    send_b = _back(core, grads, _swap(grads), wg, wu, wg_p, wu_p)
    recv_b = _exchange(send_b)

    g_down = _dot_tn(hidden, e).astype(BF)
    g_gate = _dot_tn(x, grads[:, :HID]).astype(BF)
    g_up = _dot_tn(x, grads[:, HID:]).astype(BF)

    mixed, inner = _local(
        _mixed_kernel,
        [_shape((BLOCK, COLS), BF), _shape((TOPK, BLOCK), F32)],
        4e8,
        3e6,
        "mixed",
        ids_t,
        pick,
        weight,
        cotangent,
        _hbm(recv_o),
    )
    inner = inner + _swap(inner)
    far = _swap(inner, "yhi")
    recv_b, g_gate, g_up, g_down = lax.optimization_barrier((recv_b, g_gate, g_up, g_down))
    grad_tokens, grad_probs = _local(
        _grad_tokens_kernel,
        [_shape((BLOCK, COLS), BF), _shape((TOPK, BLOCK), F32)],
        2e8,
        3e6,
        "grad_tokens",
        pick,
        recv_b,
        inner,
        far,
    )
    return mixed, grad_tokens, grad_probs.T, g_gate[None], g_up[None], g_down[None]


def solution(mesh):
    fine = Mesh(mesh.devices.reshape(EXPERTS, 2, 2), ("expert", "yhi", "core"))
    dp = ("yhi", "core")
    return jax.shard_map(
        body,
        mesh=fine,
        in_specs=(
            P("expert", dp),
            P("expert", dp),
            P("expert", None),
            P("expert", None),
            P("expert", None, dp),
            P("expert", None, dp),
            P("expert", dp, None),
        ),
        out_specs=(
            P("expert", dp),
            P("expert", dp),
            P("expert", None),
            P("expert", None, dp),
            P("expert", None, dp),
            P("expert", dp, None),
        ),
        check_vma=False,
    )
```

```python
import functools

import jax
import jax.numpy as jnp
from jax import lax
from jax.experimental import pallas as pl
from jax.experimental.pallas import tpu as pltpu
from jax.sharding import Mesh, PartitionSpec as P

BF = jnp.bfloat16
F32 = jnp.float32

EXPERTS = 32
BLOCK = 128
TOPK = 6
COLS = 1280
HALF = 640
HID = 384
ROWS = 384
MAIN = 256
REST = 128
WIDE = COLS + HALF
D = 4 * COLS
VMEM = 40 * 1024 * 1024
EARLY = 16
LATE = 1 / 128


def _dot(a, b):
    return jnp.dot(a, b, preferred_element_type=F32)


def _dot_nt(a, b):
    return lax.dot_general(a, b, (((1,), (1,)), ((), ())), preferred_element_type=F32)


def _dot_tn(a, b):
    return lax.dot_general(a, b, (((0,), (0,)), ((), ())), preferred_element_type=F32)


def _iota(shape, dim):
    return lax.broadcasted_iota(jnp.int32, shape, dim)


def _routing(ids_t, probs_t):
    expert = _iota((EXPERTS, BLOCK), 0)
    chosen = jnp.zeros((EXPERTS, BLOCK), F32)
    weight = jnp.zeros((EXPERTS, BLOCK), F32)
    for k in range(TOPK):
        hit = ids_t[k : k + 1, :] == expert
        chosen = jnp.where(hit, 1.0, chosen)
        weight = jnp.where(hit, probs_t[k : k + 1, :], weight)
    earlier = (_iota((BLOCK, BLOCK), 0) < _iota((BLOCK, BLOCK), 1)).astype(F32).astype(BF)
    before = _dot(chosen.astype(BF), earlier)
    code = jnp.where(chosen > 0.5, before, -1.0)
    row = _iota((MAIN, EXPERTS), 0)
    spread = ((row // 8) == _iota((MAIN, EXPERTS), 1)).astype(F32).astype(BF)
    place = _dot(spread, code.astype(BF))
    j = _iota((MAIN, BLOCK), 0)
    main = jnp.where(place == (j % 8).astype(F32), 1.0, 0.0)
    rest = jnp.where(place == (8 + j % 4).astype(F32), 1.0, 0.0)
    hi = weight.astype(BF)
    left = weight - hi.astype(F32)
    mid = left.astype(BF)
    low = (left - mid.astype(F32)).astype(BF)
    full = _dot(spread, hi) + _dot(spread, mid) + _dot(spread, low)
    return main, rest, full


def _lower_half(shape):
    return (_iota(shape, 0) % 8) < 4


def _send(main, rest, source):
    first = _lower_half((MAIN, BLOCK))
    p0 = jnp.where(first, rest, 0.0).astype(BF)
    p1 = jnp.where(first, 0.0, rest).astype(BF)
    a = _dot(main.astype(BF), source)
    b = _dot(p0, source[:, :HALF]) + _dot(p1, source[:, HALF:])
    return a, b


def _pack_rows_kernel(ids_ref, probs_ref, tok_ref, out_ref):
    main, rest, _ = _routing(ids_ref[...], probs_ref[...])
    a, b = _send(main, rest, tok_ref[...])
    a, b = a.astype(BF), b.astype(BF)
    for y in range(2):
        out_ref[y, :, :COLS] = a
        out_ref[y, :, COLS:] = b


def _pack_grads_kernel(ids_ref, probs_ref, cot_ref, out_ref, pick_ref, weight_ref):
    main, rest, full = _routing(ids_ref[...], probs_ref[...])
    a, b = _send(main, rest, cot_ref[...])
    wm, wr = main * full, rest * full
    a = (a * jnp.sum(wm, axis=1, keepdims=True)).astype(BF)
    b = (b * jnp.sum(wr, axis=1, keepdims=True)).astype(BF)
    for y in range(2):
        out_ref[y, :, :COLS] = a
        out_ref[y, :, COLS:] = b
    pick_ref[:MAIN, :] = main.astype(BF)
    pick_ref[MAIN:, :] = rest.astype(BF)
    weight_ref[:MAIN, :] = wm
    weight_ref[MAIN:, :] = wr


def _fold(h):
    q = _iota((REST, MAIN), 0)
    return (_iota((REST, MAIN), 1) == (q // 4) * 8 + 4 * h + q % 4).astype(F32).astype(BF)


def _fold_t(h):
    q = _iota((MAIN, REST), 1)
    return (_iota((MAIN, REST), 0) == (q // 4) * 8 + 4 * h + q % 4).astype(F32).astype(BF)


def _unpack(r_ref, x_ref):
    rest = r_ref[0, :, COLS:]
    x_ref[:MAIN, :] = r_ref[0, :, :COLS]
    x_ref[MAIN:, :HALF] = _dot(_fold(0), rest).astype(BF)
    x_ref[MAIN:, HALF:] = _dot(_fold(1), rest).astype(BF)


def _pack(value, out_ref):
    rest = value[MAIN:, :]
    out_ref[0, :, :COLS] = value[:MAIN, :]
    out_ref[0, :, COLS:] = (_dot(_fold_t(0), rest[:, :HALF]) + _dot(_fold_t(1), rest[:, HALF:])).astype(BF)


def _forward_own_kernel(core_ref, r_ref, wg_ref, wu_ref, x_ref, g_ref, u_ref):
    _unpack(r_ref, x_ref)
    g = _dot(x_ref[...], wg_ref[...])
    u = _dot(x_ref[...], wu_ref[...])

    @pl.when(pl.program_id(0) == 0)
    def _():
        g_ref[...] = g
        u_ref[...] = u

    @pl.when(pl.program_id(0) > 0)
    def _():
        g_ref[...] += g
        u_ref[...] += u


def _forward_other_kernel(core_ref, r_ref, wg_ref, wu_ref, g0_ref, u0_ref, x0_ref, x_ref, g_ref, u_ref, h_ref):
    _unpack(r_ref, x_ref)
    g = _dot(x_ref[...], wg_ref[...])
    u = _dot(x_ref[...], wu_ref[...])

    @pl.when(pl.program_id(0) == 0)
    def _():
        g_ref[...] = g0_ref[...] + g
        u_ref[...] = u0_ref[...] + u

    @pl.when(pl.program_id(0) > 0)
    def _():
        gate = g_ref[...] + g
        up = u_ref[...] + u
        g_ref[...] = gate
        u_ref[...] = up
        h_ref[...] = (gate * jax.nn.sigmoid(gate) * up).astype(BF)


def _backward_own_kernel(core_ref, r_ref, wd_ref, e_ref, a_ref):
    _unpack(r_ref, e_ref)
    a = _dot_nt(e_ref[...], wd_ref[...])

    @pl.when(pl.program_id(0) == 0)
    def _():
        a_ref[...] = a

    @pl.when(pl.program_id(0) > 0)
    def _():
        a_ref[...] += a


def _backward_other_kernel(core_ref, r_ref, wd_ref, a0_ref, g_ref, u_ref, e0_ref, e_ref, d_ref, a_ref):
    _unpack(r_ref, e_ref)
    a = _dot_nt(e_ref[...], wd_ref[...])

    @pl.when(pl.program_id(0) == 0)
    def _():
        a_ref[...] = a0_ref[...] + a

    @pl.when(pl.program_id(0) > 0)
    def _():
        total, gate = a_ref[...] + a, g_ref[...]
        s = jax.nn.sigmoid(gate)
        d_ref[:, :HID] = (total * u_ref[...] * s * (1.0 + gate * (1.0 - s))).astype(BF)
        d_ref[:, HID:] = (total * (gate * s)).astype(BF)


def _result_kernel(core_ref, h_ref, hp_ref, wd_ref, wdp_ref, out_ref):
    value = _dot(h_ref[...], wd_ref[...]) + _dot(hp_ref[...], wdp_ref[...])
    _pack(value.astype(BF), out_ref)


def _back_kernel(core_ref, d_ref, dp_ref, wg_ref, wu_ref, wgp_ref, wup_ref, out_ref):
    value = _dot_nt(d_ref[:, :HID], wg_ref[...]) + _dot_nt(d_ref[:, HID:], wu_ref[...])
    value += _dot_nt(dp_ref[:, :HID], wgp_ref[...]) + _dot_nt(dp_ref[:, HID:], wup_ref[...])
    _pack(value.astype(BF), out_ref)


def _home(pick, r_ref):
    main = pick[:MAIN, :]
    first = _lower_half((MAIN, BLOCK))
    rest = pick[MAIN:, :].astype(F32)
    halves = (jnp.where(first, rest, 0.0).astype(BF), jnp.where(first, 0.0, rest).astype(BF))
    out = []
    for h in range(2):
        total = jnp.zeros((BLOCK, HALF), F32)
        for y in range(2):
            total += _dot_tn(main, r_ref[y, :, h * HALF : (h + 1) * HALF])
            total += _dot_tn(halves[h], r_ref[y, :, COLS:])
        out.append(total)
    return out


def _mixed_kernel(ids_ref, pick_ref, weight_ref, cot_ref, r_ref, mixed_ref, gp_ref):
    w = weight_ref[...]
    hi = w.astype(BF)
    lo = (w - hi.astype(F32)).astype(BF)
    top, bottom = _home(hi, r_ref), _home(lo, r_ref)
    for h in range(2):
        mixed_ref[:, h * HALF : (h + 1) * HALF] = (top[h] + bottom[h]).astype(BF)
    cot = cot_ref[...]
    first = _lower_half((MAIN, BLOCK))
    inner = jnp.zeros((MAIN, BLOCK), F32)
    inner_rest = jnp.zeros((MAIN, BLOCK), F32)
    for y in range(2):
        inner += _dot_nt(r_ref[y, :, :COLS], cot)
        rest = r_ref[y, :, COLS:]
        inner_rest += jnp.where(first, _dot_nt(rest, cot[:, :HALF]), _dot_nt(rest, cot[:, HALF:]))
    pick = pick_ref[...].astype(F32)
    both = pick[:MAIN, :] * inner + pick[MAIN:, :] * inner_rest
    each = jnp.sum(both.reshape(EXPERTS, 8, BLOCK), axis=1)
    expert = _iota((EXPERTS, BLOCK), 0)
    ids = ids_ref[...]
    for k in range(TOPK):
        gp_ref[k : k + 1, :] = jnp.sum(jnp.where(ids[k : k + 1, :] == expert, each, 0.0), axis=0, keepdims=True)


def _grad_tokens_kernel(pick_ref, r_ref, inner_ref, far_ref, out_ref, gp_ref):
    gp_ref[...] = inner_ref[...] + far_ref[...]
    halves = _home(pick_ref[...], r_ref)
    for h in range(2):
        out_ref[:, h * HALF : (h + 1) * HALF] = halves[h].astype(BF)


def _params():
    return pltpu.CompilerParams(vmem_limit_bytes=VMEM)


def _cost(flops, moved):
    return pl.CostEstimate(flops=int(flops), bytes_accessed=int(moved), transcendentals=0)


def _shape(shape, dtype):
    return jax.ShapeDtypeStruct(shape, dtype)


def _hbm(value):
    return pltpu.with_memory_space_constraint(value, pltpu.HBM)


def _fixed(*shape):
    return pl.BlockSpec(shape, lambda i, c: (0,) * len(shape))


def _half_pass(kernel, other, weights, state, out, scratch, flops, moved, name, aliases={}):
    def group(i, c):
        return 2 * i + (1 - c[0] if other else c[0])

    block = {
        "row": pl.BlockSpec((COLS, HID), lambda i, c: (group(i, c), 0)),
        "column": pl.BlockSpec((HID, COLS), lambda i, c: (0, group(i, c))),
        "received": pl.BlockSpec((1, MAIN, WIDE), lambda i, c: (i, 0, 0)),
        "slots": pl.BlockSpec((ROWS, COLS), lambda i, c: (0, group(i, c))),
        "whole": pl.BlockSpec(memory_space=pl.ANY),
        "hidden": _fixed(ROWS, HID),
        "both": _fixed(ROWS, 2 * HID),
    }
    return pl.pallas_call(
        kernel,
        grid_spec=pltpu.PrefetchScalarGridSpec(
            num_scalar_prefetch=1,
            grid=(2,),
            in_specs=[block["received"]] + [block[k] for k in weights + state],
            out_specs=[block[k] for k, _ in out],
            scratch_shapes=scratch,
        ),
        out_shape=[t for _, t in out],
        input_output_aliases=aliases,
        compiler_params=_params(),
        cost_estimate=_cost(flops, moved),
        name=name,
    )


def _forward_own(core, own, w_gate, w_up):
    return _half_pass(
        _forward_own_kernel,
        False,
        ["row", "row"],
        [],
        [("slots", pltpu.HBM((ROWS, D), BF)), ("hidden", _shape((ROWS, HID), F32)), ("hidden", _shape((ROWS, HID), F32))],
        [],
        EARLY * 2 * ROWS * D * HID,
        EARLY * 9e6,
        "forward_own",
    )(core, _hbm(own), _hbm(w_gate), _hbm(w_up))


def _forward_other(core, other, w_gate, w_up, gate, up, x):
    return _half_pass(
        _forward_other_kernel,
        True,
        ["row", "row"],
        ["hidden", "hidden", "whole"],
        [
            ("slots", pltpu.HBM((ROWS, D), BF)),
            ("hidden", _shape((ROWS, HID), F32)),
            ("hidden", _shape((ROWS, HID), F32)),
            ("hidden", _shape((ROWS, HID), BF)),
        ],
        [],
        LATE * 2 * ROWS * D * HID,
        LATE * 9e6,
        "forward_other",
        {6: 0},
    )(core, _hbm(other), _hbm(w_gate), _hbm(w_up), gate, up, _hbm(x))


def _backward_own(core, own, w_down):
    return _half_pass(
        _backward_own_kernel,
        False,
        ["column"],
        [],
        [("slots", pltpu.HBM((ROWS, D), BF)), ("hidden", _shape((ROWS, HID), F32))],
        [],
        EARLY * 2 * ROWS * D * HID,
        EARLY * 9e6,
        "backward_own",
    )(core, _hbm(own), _hbm(w_down))


def _backward_other(core, other, w_down, partial, gate, up, e):
    return _half_pass(
        _backward_other_kernel,
        True,
        ["column"],
        ["hidden", "hidden", "hidden", "whole"],
        [("slots", pltpu.HBM((ROWS, D), BF)), ("both", _shape((ROWS, 2 * HID), BF))],
        [pltpu.VMEM((ROWS, HID), F32)],
        LATE * ROWS * D * HID,
        LATE * 6e6,
        "backward_other",
        {6: 0},
    )(core, _hbm(other), _hbm(w_down), partial, gate, up, _hbm(e))


def _result(core, hidden, hidden_p, w_down, w_down_p):
    weight = pl.BlockSpec((HID, COLS), lambda i, c: (0, 2 * i + c[0]))
    return pl.pallas_call(
        _result_kernel,
        grid_spec=pltpu.PrefetchScalarGridSpec(
            num_scalar_prefetch=1,
            grid=(2,),
            in_specs=[_fixed(ROWS, HID), _fixed(ROWS, HID), weight, weight],
            out_specs=pl.BlockSpec((1, MAIN, WIDE), lambda i, c: (i, 0, 0)),
        ),
        out_shape=pltpu.HBM((2, MAIN, WIDE), BF),
        compiler_params=_params(),
        cost_estimate=_cost(LATE * 2 * ROWS * D * HID, LATE * 7e6),
        name="result",
    )(core, hidden, hidden_p, _hbm(w_down), _hbm(w_down_p))


def _back(core, grads, grads_p, w_gate, w_up, w_gate_p, w_up_p):
    weight = pl.BlockSpec((COLS, HID), lambda i, c: (2 * i + c[0], 0))
    return pl.pallas_call(
        _back_kernel,
        grid_spec=pltpu.PrefetchScalarGridSpec(
            num_scalar_prefetch=1,
            grid=(2,),
            in_specs=[_fixed(ROWS, 2 * HID), _fixed(ROWS, 2 * HID), weight, weight, weight, weight],
            out_specs=pl.BlockSpec((1, MAIN, WIDE), lambda i, c: (i, 0, 0)),
        ),
        out_shape=pltpu.HBM((2, MAIN, WIDE), BF),
        compiler_params=_params(),
        cost_estimate=_cost(LATE * 4 * ROWS * D * HID, LATE * 11e6),
        name="back",
    )(core, grads, grads_p, _hbm(w_gate), _hbm(w_up), _hbm(w_gate_p), _hbm(w_up_p))


def _local(kernel, out_shape, flops, moved, name, *args):
    return pl.pallas_call(
        kernel, out_shape=out_shape, compiler_params=_params(), cost_estimate=_cost(flops, moved), name=name
    )(*args)


def _exchange(packed):
    chunks = packed.reshape(2 * EXPERTS, 8, WIDE)
    got = lax.all_to_all(chunks, ("yhi", "expert"), split_axis=0, concat_axis=0, tiled=True)
    return got.reshape(2, MAIN, WIDE)


def _swap(value, axis="core"):
    return lax.ppermute(value, axis, [(0, 1), (1, 0)])


def body(tokens, cotangent, expert_ids, route_probs, w_gate, w_up, w_down):
    core = lax.axis_index("core").astype(jnp.int32).reshape(1)
    wg, wu, wd = w_gate[0], w_up[0], w_down[0]
    ids_t, probs_t = expert_ids.T, route_probs.T

    send_x = _local(_pack_rows_kernel, pltpu.HBM((2, MAIN, WIDE), BF), 2e8, 3e6, "pack_rows", _hbm(ids_t), _hbm(probs_t), _hbm(tokens))
    recv_x = _exchange(send_x)
    send_e, pick, weight = _local(
        _pack_grads_kernel,
        [pltpu.HBM((2, MAIN, WIDE), BF), _shape((2 * MAIN, BLOCK), BF), _shape((2 * MAIN, BLOCK), F32)],
        2e8,
        3e6,
        "pack_grads",
        _hbm(ids_t),
        _hbm(probs_t),
        _hbm(cotangent),
    )
    wd_p, wg_p, wu_p = _swap(wd), _swap(wg), _swap(wu)
    recv_x, send_e = lax.optimization_barrier((recv_x, send_e))
    recv_e = _exchange(send_e)

    x, gate, up = _forward_own(core, recv_x, wg, wu)
    x, gate, up, hidden = _forward_other(core, _swap(recv_x), wg, wu, gate, up, x)
    send_o = _result(core, hidden, _swap(hidden), wd, wd_p)
    recv_e, send_o = lax.optimization_barrier((recv_e, send_o))
    recv_o = _exchange(send_o)

    e, partial = _backward_own(core, recv_e, wd)
    e, grads = _backward_other(core, _swap(recv_e), wd, partial, gate, up, e)
    send_b = _back(core, grads, _swap(grads), wg, wu, wg_p, wu_p)
    recv_b = _exchange(send_b)

    g_down = _dot_tn(hidden, e).astype(BF)
    g_gate = _dot_tn(x, grads[:, :HID]).astype(BF)
    g_up = _dot_tn(x, grads[:, HID:]).astype(BF)

    mixed, inner = _local(
        _mixed_kernel,
        [_shape((BLOCK, COLS), BF), _shape((TOPK, BLOCK), F32)],
        4e8,
        3e6,
        "mixed",
        _hbm(ids_t),
        _hbm(pick),
        _hbm(weight),
        _hbm(cotangent),
        _hbm(recv_o),
    )
    inner = inner + _swap(inner)
    far = _swap(inner, "yhi")
    recv_b, g_gate, g_up, g_down = lax.optimization_barrier((recv_b, g_gate, g_up, g_down))
    grad_tokens, grad_probs = _local(
        _grad_tokens_kernel,
        [_shape((BLOCK, COLS), BF), _shape((TOPK, BLOCK), F32)],
        2e8,
        3e6,
        "grad_tokens",
        pick,
        recv_b,
        inner,
        far,
    )
    return mixed, grad_tokens, grad_probs.T, g_gate[None], g_up[None], g_down[None]


def solution(mesh):
    fine = Mesh(mesh.devices.reshape(EXPERTS, 2, 2), ("expert", "yhi", "core"))
    dp = ("yhi", "core")
    return jax.shard_map(
        body,
        mesh=fine,
        in_specs=(
            P("expert", dp),
            P("expert", dp),
            P("expert", None),
            P("expert", None),
            P("expert", None, dp),
            P("expert", None, dp),
            P("expert", dp, None),
        ),
        out_specs=(
            P("expert", dp),
            P("expert", dp),
            P("expert", None),
            P("expert", None, dp),
            P("expert", None, dp),
            P("expert", dp, None),
        ),
        check_vma=False,
    )
```

```python
import functools

import jax
import jax.numpy as jnp
from jax import lax
from jax.experimental import pallas as pl
from jax.experimental.pallas import tpu as pltpu
from jax.sharding import Mesh, PartitionSpec as P

BF = jnp.bfloat16
F32 = jnp.float32

EXPERTS = 32
BLOCK = 128
TOPK = 6
COLS = 1280
HALF = 640
HID = 384
ROWS = 384
MAIN = 256
REST = 128
STEPS = 4
WIDE = COLS + HALF
D = 4 * COLS
VMEM = 40 * 1024 * 1024
EARLY = 16
LATE = 1 / 128


def _dot(a, b):
    return jnp.dot(a, b, preferred_element_type=F32)


def _dot_nt(a, b):
    return lax.dot_general(a, b, (((1,), (1,)), ((), ())), preferred_element_type=F32)


def _dot_tn(a, b):
    return lax.dot_general(a, b, (((0,), (0,)), ((), ())), preferred_element_type=F32)


def _iota(shape, dim):
    return lax.broadcasted_iota(jnp.int32, shape, dim)


def _routing(ids_t, probs_t=None):
    expert = _iota((EXPERTS, BLOCK), 0)
    chosen = jnp.zeros((EXPERTS, BLOCK), F32)
    weight = jnp.zeros((EXPERTS, BLOCK), F32)
    for k in range(TOPK):
        hit = ids_t[k : k + 1, :] == expert
        chosen = jnp.where(hit, 1.0, chosen)
        if probs_t is not None:
            weight = jnp.where(hit, probs_t[k : k + 1, :], weight)
    earlier = (_iota((BLOCK, BLOCK), 0) < _iota((BLOCK, BLOCK), 1)).astype(F32).astype(BF)
    before = _dot(chosen.astype(BF), earlier)
    code = jnp.where(chosen > 0.5, before, -1.0)
    row = _iota((MAIN, EXPERTS), 0)
    spread = ((row // 8) == _iota((MAIN, EXPERTS), 1)).astype(F32).astype(BF)
    place = _dot(spread, code.astype(BF))
    j = _iota((MAIN, BLOCK), 0)
    main = jnp.where(place == (j % 8).astype(F32), 1.0, 0.0)
    rest = jnp.where(place == (8 + j % 4).astype(F32), 1.0, 0.0)
    if probs_t is None:
        return main, rest, None
    hi = weight.astype(BF)
    left = weight - hi.astype(F32)
    mid = left.astype(BF)
    low = (left - mid.astype(F32)).astype(BF)
    full = _dot(spread, hi) + _dot(spread, mid) + _dot(spread, low)
    return main, rest, full


def _lower_half(shape):
    return (_iota(shape, 0) % 8) < 4


def _send(main, rest, source):
    first = _lower_half((MAIN, BLOCK))
    p0 = jnp.where(first, rest, 0.0).astype(BF)
    p1 = jnp.where(first, 0.0, rest).astype(BF)
    a = _dot(main.astype(BF), source)
    b = _dot(p0, source[:, :HALF]) + _dot(p1, source[:, HALF:])
    return a, b


def _pack_rows_kernel(ids_ref, tok_ref, out_ref):
    main, rest, _ = _routing(ids_ref[...])
    a, b = _send(main, rest, tok_ref[...])
    a, b = a.astype(BF), b.astype(BF)
    for y in range(2):
        out_ref[y, :, :COLS] = a
        out_ref[y, :, COLS:] = b


def _pack_grads_kernel(ids_ref, probs_ref, cot_ref, out_ref, pick_ref, weight_ref):
    main, rest, full = _routing(ids_ref[...], probs_ref[...])
    a, b = _send(main, rest, cot_ref[...])
    wm, wr = main * full, rest * full
    a = (a * jnp.sum(wm, axis=1, keepdims=True)).astype(BF)
    b = (b * jnp.sum(wr, axis=1, keepdims=True)).astype(BF)
    for y in range(2):
        out_ref[y, :, :COLS] = a
        out_ref[y, :, COLS:] = b
    pick_ref[:MAIN, :] = main.astype(BF)
    pick_ref[MAIN:, :] = rest.astype(BF)
    weight_ref[:MAIN, :] = wm
    weight_ref[MAIN:, :] = wr


def _fold(h):
    q = _iota((REST, MAIN), 0)
    return (_iota((REST, MAIN), 1) == (q // 4) * 8 + 4 * h + q % 4).astype(F32).astype(BF)


def _fold_t(h):
    q = _iota((MAIN, REST), 1)
    return (_iota((MAIN, REST), 0) == (q // 4) * 8 + 4 * h + q % 4).astype(F32).astype(BF)


def _unpack(main_ref, rest_ref, x_ref):
    x_ref[:MAIN, :] = main_ref[0]
    x_ref[MAIN:, :] = _dot(_fold(pl.program_id(0) % 2), rest_ref[0]).astype(BF)


def _pack(value, out_ref):
    h = pl.program_id(0) % 2
    rest = _dot(_fold_t(h), value[MAIN:, :]).astype(BF)

    @pl.when(h == 0)
    def _():
        out_ref[0, :, :HALF] = value[:MAIN, :]
        out_ref[0, :, COLS:] = rest

    @pl.when(h == 1)
    def _():
        out_ref[0, :, HALF:COLS] = value[:MAIN, :]
        out_ref[0, :, COLS:] += rest


def _forward_own_kernel(core_ref, main_ref, rest_ref, wg_ref, wu_ref, x_ref, g_ref, u_ref):
    _unpack(main_ref, rest_ref, x_ref)
    g = _dot(x_ref[...], wg_ref[...])
    u = _dot(x_ref[...], wu_ref[...])

    @pl.when(pl.program_id(0) == 0)
    def _():
        g_ref[...] = g
        u_ref[...] = u

    @pl.when(pl.program_id(0) > 0)
    def _():
        g_ref[...] += g
        u_ref[...] += u


def _forward_other_kernel(core_ref, main_ref, rest_ref, wg_ref, wu_ref, g0_ref, u0_ref, x0_ref, x_ref, g_ref, u_ref, h_ref):
    _unpack(main_ref, rest_ref, x_ref)
    g = _dot(x_ref[...], wg_ref[...])
    u = _dot(x_ref[...], wu_ref[...])

    @pl.when(pl.program_id(0) == 0)
    def _():
        g_ref[...] = g0_ref[...] + g
        u_ref[...] = u0_ref[...] + u

    @pl.when(pl.program_id(0) > 0)
    def _():
        g_ref[...] += g
        u_ref[...] += u

    @pl.when(pl.program_id(0) == STEPS - 1)
    def _():
        gate, up = g_ref[...], u_ref[...]
        h_ref[...] = (gate * jax.nn.sigmoid(gate) * up).astype(BF)


def _backward_own_kernel(core_ref, main_ref, rest_ref, wd_ref, e_ref, a_ref):
    _unpack(main_ref, rest_ref, e_ref)
    a = _dot_nt(e_ref[...], wd_ref[...])

    @pl.when(pl.program_id(0) == 0)
    def _():
        a_ref[...] = a

    @pl.when(pl.program_id(0) > 0)
    def _():
        a_ref[...] += a


def _backward_other_kernel(core_ref, main_ref, rest_ref, wd_ref, a0_ref, g_ref, u_ref, e0_ref, e_ref, d_ref, a_ref):
    _unpack(main_ref, rest_ref, e_ref)
    a = _dot_nt(e_ref[...], wd_ref[...])

    @pl.when(pl.program_id(0) == 0)
    def _():
        a_ref[...] = a0_ref[...] + a

    @pl.when(pl.program_id(0) > 0)
    def _():
        a_ref[...] += a

    @pl.when(pl.program_id(0) == STEPS - 1)
    def _():
        total, gate = a_ref[...], g_ref[...]
        s = jax.nn.sigmoid(gate)
        d_ref[:, :HID] = (total * u_ref[...] * s * (1.0 + gate * (1.0 - s))).astype(BF)
        d_ref[:, HID:] = (total * (gate * s)).astype(BF)


def _result_kernel(core_ref, h_ref, hp_ref, wd_ref, wdp_ref, out_ref):
    value = _dot(h_ref[...], wd_ref[...]) + _dot(hp_ref[...], wdp_ref[...])
    _pack(value.astype(BF), out_ref)


def _back_kernel(core_ref, d_ref, dp_ref, wg_ref, wu_ref, wgp_ref, wup_ref, out_ref):
    value = _dot_nt(d_ref[:, :HID], wg_ref[...]) + _dot_nt(d_ref[:, HID:], wu_ref[...])
    value += _dot_nt(dp_ref[:, :HID], wgp_ref[...]) + _dot_nt(dp_ref[:, HID:], wup_ref[...])
    _pack(value.astype(BF), out_ref)


def _home(pick, r_ref):
    main = pick[:MAIN, :]
    first = _lower_half((MAIN, BLOCK))
    rest = pick[MAIN:, :].astype(F32)
    halves = (jnp.where(first, rest, 0.0).astype(BF), jnp.where(first, 0.0, rest).astype(BF))
    out = []
    for h in range(2):
        total = jnp.zeros((BLOCK, HALF), F32)
        for y in range(2):
            total += _dot_tn(main, r_ref[y, :, h * HALF : (h + 1) * HALF])
            total += _dot_tn(halves[h], r_ref[y, :, COLS:])
        out.append(total)
    return out


def _mixed_kernel(ids_ref, pick_ref, weight_ref, cot_ref, r_ref, mixed_ref, gp_ref):
    w = weight_ref[...]
    hi = w.astype(BF)
    lo = (w - hi.astype(F32)).astype(BF)
    top, bottom = _home(hi, r_ref), _home(lo, r_ref)
    for h in range(2):
        mixed_ref[:, h * HALF : (h + 1) * HALF] = (top[h] + bottom[h]).astype(BF)
    cot = cot_ref[...]
    first = _lower_half((MAIN, BLOCK))
    inner = jnp.zeros((MAIN, BLOCK), F32)
    inner_rest = jnp.zeros((MAIN, BLOCK), F32)
    for y in range(2):
        inner += _dot_nt(r_ref[y, :, :COLS], cot)
        rest = r_ref[y, :, COLS:]
        inner_rest += jnp.where(first, _dot_nt(rest, cot[:, :HALF]), _dot_nt(rest, cot[:, HALF:]))
    pick = pick_ref[...].astype(F32)
    both = pick[:MAIN, :] * inner + pick[MAIN:, :] * inner_rest
    each = jnp.sum(both.reshape(EXPERTS, 8, BLOCK), axis=1)
    expert = _iota((EXPERTS, BLOCK), 0)
    ids = ids_ref[...]
    for k in range(TOPK):
        gp_ref[k : k + 1, :] = jnp.sum(jnp.where(ids[k : k + 1, :] == expert, each, 0.0), axis=0, keepdims=True)


def _grad_tokens_kernel(pick_ref, r_ref, inner_ref, far_ref, out_ref, gp_ref):
    gp_ref[...] = inner_ref[...] + far_ref[...]
    halves = _home(pick_ref[...], r_ref)
    for h in range(2):
        out_ref[:, h * HALF : (h + 1) * HALF] = halves[h].astype(BF)


def _params():
    return pltpu.CompilerParams(vmem_limit_bytes=VMEM)


def _cost(flops, moved):
    return pl.CostEstimate(flops=int(flops), bytes_accessed=int(moved), transcendentals=0)


def _shape(shape, dtype):
    return jax.ShapeDtypeStruct(shape, dtype)


def _hbm(value):
    return pltpu.with_memory_space_constraint(value, pltpu.HBM)


def _fixed(*shape):
    return pl.BlockSpec(shape, lambda i, c: (0,) * len(shape))


def _piece(i, core):
    return (2 * (i // 2) + core) * 2 + i % 2


def _half_pass(kernel, other, weights, state, out, scratch, flops, moved, name, aliases={}):
    def piece(i, c):
        return _piece(i, 1 - c[0] if other else c[0])

    block = {
        "row": pl.BlockSpec((HALF, HID), lambda i, c: (piece(i, c), 0)),
        "column": pl.BlockSpec((HID, HALF), lambda i, c: (0, piece(i, c))),
        "main": pl.BlockSpec((1, MAIN, HALF), lambda i, c: (i // 2, 0, i % 2)),
        "rest": pl.BlockSpec((1, MAIN, HALF), lambda i, c: (i // 2, 0, 2)),
        "slots": pl.BlockSpec((ROWS, HALF), lambda i, c: (0, piece(i, c))),
        "whole": pl.BlockSpec(memory_space=pl.ANY),
        "hidden": _fixed(ROWS, HID),
        "both": _fixed(ROWS, 2 * HID),
    }
    return pl.pallas_call(
        kernel,
        grid_spec=pltpu.PrefetchScalarGridSpec(
            num_scalar_prefetch=1,
            grid=(STEPS,),
            in_specs=[block[k] for k in ("main", "rest")] + [block[k] for k in weights + state],
            out_specs=[block[k] for k, _ in out],
            scratch_shapes=scratch,
        ),
        out_shape=[t for _, t in out],
        input_output_aliases=aliases,
        compiler_params=_params(),
        cost_estimate=_cost(flops, moved),
        name=name,
    )


def _forward_own(core, own, w_gate, w_up):
    return _half_pass(
        _forward_own_kernel,
        False,
        ["row", "row"],
        [],
        [("slots", pltpu.HBM((ROWS, D), BF)), ("hidden", _shape((ROWS, HID), F32)), ("hidden", _shape((ROWS, HID), F32))],
        [],
        EARLY * 2 * ROWS * D * HID,
        EARLY * 9e6,
        "forward_own",
    )(core, _hbm(own), _hbm(own), _hbm(w_gate), _hbm(w_up))


def _forward_other(core, other, w_gate, w_up, gate, up, x):
    return _half_pass(
        _forward_other_kernel,
        True,
        ["row", "row"],
        ["hidden", "hidden", "whole"],
        [
            ("slots", pltpu.HBM((ROWS, D), BF)),
            ("hidden", _shape((ROWS, HID), F32)),
            ("hidden", _shape((ROWS, HID), F32)),
            ("hidden", _shape((ROWS, HID), BF)),
        ],
        [],
        LATE * 2 * ROWS * D * HID,
        LATE * 9e6,
        "forward_other",
        {7: 0},
    )(core, other, other, _hbm(w_gate), _hbm(w_up), gate, up, _hbm(x))


def _backward_own(core, own, w_down):
    return _half_pass(
        _backward_own_kernel,
        False,
        ["column"],
        [],
        [("slots", pltpu.HBM((ROWS, D), BF)), ("hidden", _shape((ROWS, HID), F32))],
        [],
        EARLY * 2 * ROWS * D * HID,
        EARLY * 9e6,
        "backward_own",
    )(core, _hbm(own), _hbm(own), _hbm(w_down))


def _backward_other(core, other, w_down, partial, gate, up, e):
    return _half_pass(
        _backward_other_kernel,
        True,
        ["column"],
        ["hidden", "hidden", "hidden", "whole"],
        [("slots", pltpu.HBM((ROWS, D), BF)), ("both", _shape((ROWS, 2 * HID), BF))],
        [pltpu.VMEM((ROWS, HID), F32)],
        LATE * ROWS * D * HID,
        LATE * 6e6,
        "backward_other",
        {7: 0},
    )(core, other, other, _hbm(w_down), partial, gate, up, _hbm(e))


def _result(core, hidden, hidden_p, w_down, w_down_p):
    weight = pl.BlockSpec((HID, HALF), lambda i, c: (0, _piece(i, c[0])))
    return pl.pallas_call(
        _result_kernel,
        grid_spec=pltpu.PrefetchScalarGridSpec(
            num_scalar_prefetch=1,
            grid=(STEPS,),
            in_specs=[_fixed(ROWS, HID), _fixed(ROWS, HID), weight, weight],
            out_specs=pl.BlockSpec((1, MAIN, WIDE), lambda i, c: (i // 2, 0, 0)),
        ),
        out_shape=pltpu.HBM((2, MAIN, WIDE), BF),
        compiler_params=_params(),
        cost_estimate=_cost(LATE * 2 * ROWS * D * HID, LATE * 7e6),
        name="result",
    )(core, hidden, hidden_p, _hbm(w_down), _hbm(w_down_p))


def _back(core, grads, grads_p, w_gate, w_up, w_gate_p, w_up_p):
    weight = pl.BlockSpec((HALF, HID), lambda i, c: (_piece(i, c[0]), 0))
    return pl.pallas_call(
        _back_kernel,
        grid_spec=pltpu.PrefetchScalarGridSpec(
            num_scalar_prefetch=1,
            grid=(STEPS,),
            in_specs=[_fixed(ROWS, 2 * HID), _fixed(ROWS, 2 * HID), weight, weight, weight, weight],
            out_specs=pl.BlockSpec((1, MAIN, WIDE), lambda i, c: (i // 2, 0, 0)),
        ),
        out_shape=pltpu.HBM((2, MAIN, WIDE), BF),
        compiler_params=_params(),
        cost_estimate=_cost(LATE * 4 * ROWS * D * HID, LATE * 11e6),
        name="back",
    )(core, grads, grads_p, _hbm(w_gate), _hbm(w_up), _hbm(w_gate_p), _hbm(w_up_p))


def _local(kernel, out_shape, flops, moved, name, *args):
    return pl.pallas_call(
        kernel, out_shape=out_shape, compiler_params=_params(), cost_estimate=_cost(flops, moved), name=name
    )(*args)


def _exchange(packed):
    chunks = packed.reshape(2 * EXPERTS, 8, WIDE)
    got = lax.all_to_all(chunks, ("yhi", "expert"), split_axis=0, concat_axis=0, tiled=True)
    return got.reshape(2, MAIN, WIDE)


def _swap(value, axis="core"):
    return lax.ppermute(value, axis, [(0, 1), (1, 0)])


def body(tokens, cotangent, expert_ids, route_probs, w_gate, w_up, w_down):
    core = lax.axis_index("core").astype(jnp.int32).reshape(1)
    wg, wu, wd = w_gate[0], w_up[0], w_down[0]
    ids_t, probs_t = expert_ids.T, route_probs.T

    send_x = _local(_pack_rows_kernel, pltpu.HBM((2, MAIN, WIDE), BF), 2e8, 3e6, "pack_rows", _hbm(ids_t), _hbm(tokens))
    recv_x = _exchange(send_x)
    send_e, pick, weight = _local(
        _pack_grads_kernel,
        [pltpu.HBM((2, MAIN, WIDE), BF), _shape((2 * MAIN, BLOCK), BF), _shape((2 * MAIN, BLOCK), F32)],
        2e8,
        3e6,
        "pack_grads",
        _hbm(ids_t),
        _hbm(probs_t),
        _hbm(cotangent),
    )
    wd_p, wg_p, wu_p = _swap(wd), _swap(wg), _swap(wu)
    recv_x, send_e = lax.optimization_barrier((recv_x, send_e))
    recv_e = _exchange(send_e)

    x, gate, up = _forward_own(core, recv_x, wg, wu)
    x, gate, up, hidden = _forward_other(core, _swap(recv_x), wg, wu, gate, up, x)
    send_o = _result(core, hidden, _swap(hidden), wd, wd_p)
    recv_e, send_o = lax.optimization_barrier((recv_e, send_o))
    recv_o = _exchange(send_o)

    e, partial = _backward_own(core, recv_e, wd)
    e, grads = _backward_other(core, _swap(recv_e), wd, partial, gate, up, e)
    send_b = _back(core, grads, _swap(grads), wg, wu, wg_p, wu_p)
    recv_b = _exchange(send_b)

    g_down = _dot_tn(hidden, e).astype(BF)
    g_gate = _dot_tn(x, grads[:, :HID]).astype(BF)
    g_up = _dot_tn(x, grads[:, HID:]).astype(BF)

    mixed, inner = _local(
        _mixed_kernel,
        [_shape((BLOCK, COLS), BF), _shape((TOPK, BLOCK), F32)],
        4e8,
        3e6,
        "mixed",
        _hbm(ids_t),
        _hbm(pick),
        _hbm(weight),
        _hbm(cotangent),
        _hbm(recv_o),
    )
    inner = inner + _swap(inner)
    far = _swap(inner, "yhi")
    recv_b, g_gate, g_up, g_down = lax.optimization_barrier((recv_b, g_gate, g_up, g_down))
    grad_tokens, grad_probs = _local(
        _grad_tokens_kernel,
        [_shape((BLOCK, COLS), BF), _shape((TOPK, BLOCK), F32)],
        2e8,
        3e6,
        "grad_tokens",
        pick,
        recv_b,
        inner,
        far,
    )
    return mixed, grad_tokens, grad_probs.T, g_gate[None], g_up[None], g_down[None]


def solution(mesh):
    fine = Mesh(mesh.devices.reshape(EXPERTS, 2, 2), ("expert", "yhi", "core"))
    dp = ("yhi", "core")
    return jax.shard_map(
        body,
        mesh=fine,
        in_specs=(
            P("expert", dp),
            P("expert", dp),
            P("expert", None),
            P("expert", None),
            P("expert", None, dp),
            P("expert", None, dp),
            P("expert", dp, None),
        ),
        out_specs=(
            P("expert", dp),
            P("expert", dp),
            P("expert", None),
            P("expert", None, dp),
            P("expert", None, dp),
            P("expert", dp, None),
        ),
        check_vma=False,
    )
```

```python
import functools

import jax
import jax.numpy as jnp
from jax import lax
from jax.experimental import pallas as pl
from jax.experimental.pallas import tpu as pltpu
from jax.sharding import Mesh, PartitionSpec as P

BF = jnp.bfloat16
F32 = jnp.float32

EXPERTS = 32
BLOCK = 128
TOPK = 6
COLS = 1280
HALF = 640
HID = 384
ROWS = 384
MAIN = 256
REST = 128
WIDE = COLS + HALF
D = 4 * COLS
VMEM = 40 * 1024 * 1024
EARLY = 16
LATE = 1 / 128


def _dot(a, b):
    return jnp.dot(a, b, preferred_element_type=F32)


def _dot_nt(a, b):
    return lax.dot_general(a, b, (((1,), (1,)), ((), ())), preferred_element_type=F32)


def _dot_tn(a, b):
    return lax.dot_general(a, b, (((0,), (0,)), ((), ())), preferred_element_type=F32)


def _iota(shape, dim):
    return lax.broadcasted_iota(jnp.int32, shape, dim)


def _routing(ids_t, probs_t=None):
    expert = _iota((EXPERTS, BLOCK), 0)
    chosen = jnp.zeros((EXPERTS, BLOCK), F32)
    weight = jnp.zeros((EXPERTS, BLOCK), F32)
    for k in range(TOPK):
        hit = ids_t[k : k + 1, :] == expert
        chosen = jnp.where(hit, 1.0, chosen)
        if probs_t is not None:
            weight = jnp.where(hit, probs_t[k : k + 1, :], weight)
    earlier = (_iota((BLOCK, BLOCK), 0) < _iota((BLOCK, BLOCK), 1)).astype(F32).astype(BF)
    before = _dot(chosen.astype(BF), earlier)
    code = jnp.where(chosen > 0.5, before, -1.0)
    row = _iota((MAIN, EXPERTS), 0)
    spread = ((row // 8) == _iota((MAIN, EXPERTS), 1)).astype(F32).astype(BF)
    place = _dot(spread, code.astype(BF))
    j = _iota((MAIN, BLOCK), 0)
    main = jnp.where(place == (j % 8).astype(F32), 1.0, 0.0)
    rest = jnp.where(place == (8 + j % 4).astype(F32), 1.0, 0.0)
    if probs_t is None:
        return main, rest, None
    hi = weight.astype(BF)
    left = weight - hi.astype(F32)
    mid = left.astype(BF)
    low = (left - mid.astype(F32)).astype(BF)
    full = _dot(spread, hi) + _dot(spread, mid) + _dot(spread, low)
    return main, rest, full


def _lower_half(shape):
    return (_iota(shape, 0) % 8) < 4


def _send(main, rest, source):
    first = _lower_half((MAIN, BLOCK))
    p0 = jnp.where(first, rest, 0.0).astype(BF)
    p1 = jnp.where(first, 0.0, rest).astype(BF)
    a = _dot(main.astype(BF), source)
    b = _dot(p0, source[:, :HALF]) + _dot(p1, source[:, HALF:])
    return a, b


def _pack_rows_kernel(ids_ref, tok_ref, out_ref):
    main, rest, _ = _routing(ids_ref[...])
    a, b = _send(main, rest, tok_ref[...])
    a, b = a.astype(BF), b.astype(BF)
    for y in range(2):
        out_ref[y, :, :COLS] = a
        out_ref[y, :, COLS:] = b


def _pack_grads_kernel(ids_ref, probs_ref, cot_ref, out_ref, pick_ref, weight_ref):
    main, rest, full = _routing(ids_ref[...], probs_ref[...])
    a, b = _send(main, rest, cot_ref[...])
    wm, wr = main * full, rest * full
    a = (a * jnp.sum(wm, axis=1, keepdims=True)).astype(BF)
    b = (b * jnp.sum(wr, axis=1, keepdims=True)).astype(BF)
    for y in range(2):
        out_ref[y, :, :COLS] = a
        out_ref[y, :, COLS:] = b
    pick_ref[:MAIN, :] = main.astype(BF)
    pick_ref[MAIN:, :] = rest.astype(BF)
    weight_ref[:MAIN, :] = wm
    weight_ref[MAIN:, :] = wr


def _fold(h):
    q = _iota((REST, MAIN), 0)
    return (_iota((REST, MAIN), 1) == (q // 4) * 8 + 4 * h + q % 4).astype(F32).astype(BF)


def _fold_t(h):
    q = _iota((MAIN, REST), 1)
    return (_iota((MAIN, REST), 0) == (q // 4) * 8 + 4 * h + q % 4).astype(F32).astype(BF)


def _unpack(r_ref, x_ref):
    rest = r_ref[0, :, COLS:]
    x_ref[:MAIN, :] = r_ref[0, :, :COLS]
    x_ref[MAIN:, :HALF] = _dot(_fold(0), rest).astype(BF)
    x_ref[MAIN:, HALF:] = _dot(_fold(1), rest).astype(BF)


def _pack(value, out_ref):
    rest = value[MAIN:, :]
    out_ref[0, :, :COLS] = value[:MAIN, :]
    out_ref[0, :, COLS:] = (_dot(_fold_t(0), rest[:, :HALF]) + _dot(_fold_t(1), rest[:, HALF:])).astype(BF)


def _forward_own_kernel(core_ref, r_ref, wg_ref, wu_ref, x_ref, g_ref, u_ref):
    _unpack(r_ref, x_ref)
    g = _dot(x_ref[...], wg_ref[...])
    u = _dot(x_ref[...], wu_ref[...])

    @pl.when(pl.program_id(0) == 0)
    def _():
        g_ref[...] = g
        u_ref[...] = u

    @pl.when(pl.program_id(0) > 0)
    def _():
        g_ref[...] += g
        u_ref[...] += u


def _forward_other_kernel(core_ref, r_ref, wg_ref, wu_ref, g0_ref, u0_ref, x0_ref, x_ref, g_ref, u_ref, h_ref):
    _unpack(r_ref, x_ref)
    g = _dot(x_ref[...], wg_ref[...])
    u = _dot(x_ref[...], wu_ref[...])

    @pl.when(pl.program_id(0) == 0)
    def _():
        g_ref[...] = g0_ref[...] + g
        u_ref[...] = u0_ref[...] + u

    @pl.when(pl.program_id(0) > 0)
    def _():
        gate = g_ref[...] + g
        up = u_ref[...] + u
        g_ref[...] = gate
        u_ref[...] = up
        h_ref[...] = (gate * jax.nn.sigmoid(gate) * up).astype(BF)


def _backward_own_kernel(core_ref, r_ref, wd_ref, e_ref, a_ref):
    _unpack(r_ref, e_ref)
    a = _dot_nt(e_ref[...], wd_ref[...])

    @pl.when(pl.program_id(0) == 0)
    def _():
        a_ref[...] = a

    @pl.when(pl.program_id(0) > 0)
    def _():
        a_ref[...] += a


def _backward_other_kernel(core_ref, r_ref, wd_ref, a0_ref, g_ref, u_ref, e0_ref, e_ref, d_ref, a_ref):
    _unpack(r_ref, e_ref)
    a = _dot_nt(e_ref[...], wd_ref[...])

    @pl.when(pl.program_id(0) == 0)
    def _():
        a_ref[...] = a0_ref[...] + a

    @pl.when(pl.program_id(0) > 0)
    def _():
        total, gate = a_ref[...] + a, g_ref[...]
        s = jax.nn.sigmoid(gate)
        d_ref[:, :HID] = (total * u_ref[...] * s * (1.0 + gate * (1.0 - s))).astype(BF)
        d_ref[:, HID:] = (total * (gate * s)).astype(BF)


def _result_kernel(core_ref, h_ref, hp_ref, wd_ref, wdp_ref, out_ref):
    value = _dot(h_ref[...], wd_ref[...]) + _dot(hp_ref[...], wdp_ref[...])
    _pack(value.astype(BF), out_ref)


def _back_kernel(core_ref, d_ref, dp_ref, wg_ref, wu_ref, wgp_ref, wup_ref, out_ref):
    value = _dot_nt(d_ref[:, :HID], wg_ref[...]) + _dot_nt(d_ref[:, HID:], wu_ref[...])
    value += _dot_nt(dp_ref[:, :HID], wgp_ref[...]) + _dot_nt(dp_ref[:, HID:], wup_ref[...])
    _pack(value.astype(BF), out_ref)


def _grad_down_kernel(h_ref, e_ref, out_ref, t_ref):
    @pl.when(pl.program_id(0) == 0)
    def _():
        t_ref[...] = h_ref[...].astype(F32).T.astype(BF)

    out_ref[...] = _dot(t_ref[...], e_ref[...]).astype(BF)


def _home(pick, r_ref):
    main = pick[:MAIN, :]
    first = _lower_half((MAIN, BLOCK))
    rest = pick[MAIN:, :].astype(F32)
    halves = (jnp.where(first, rest, 0.0).astype(BF), jnp.where(first, 0.0, rest).astype(BF))
    out = []
    for h in range(2):
        total = jnp.zeros((BLOCK, HALF), F32)
        for y in range(2):
            total += _dot_tn(main, r_ref[y, :, h * HALF : (h + 1) * HALF])
            total += _dot_tn(halves[h], r_ref[y, :, COLS:])
        out.append(total)
    return out


def _mixed_kernel(ids_ref, pick_ref, weight_ref, cot_ref, r_ref, mixed_ref, gp_ref):
    w = weight_ref[...]
    hi = w.astype(BF)
    lo = (w - hi.astype(F32)).astype(BF)
    top, bottom = _home(hi, r_ref), _home(lo, r_ref)
    for h in range(2):
        mixed_ref[:, h * HALF : (h + 1) * HALF] = (top[h] + bottom[h]).astype(BF)
    cot = cot_ref[...]
    first = _lower_half((MAIN, BLOCK))
    inner = jnp.zeros((MAIN, BLOCK), F32)
    inner_rest = jnp.zeros((MAIN, BLOCK), F32)
    for y in range(2):
        inner += _dot_nt(r_ref[y, :, :COLS], cot)
        rest = r_ref[y, :, COLS:]
        inner_rest += jnp.where(first, _dot_nt(rest, cot[:, :HALF]), _dot_nt(rest, cot[:, HALF:]))
    pick = pick_ref[...].astype(F32)
    both = pick[:MAIN, :] * inner + pick[MAIN:, :] * inner_rest
    each = jnp.sum(both.reshape(EXPERTS, 8, BLOCK), axis=1)
    expert = _iota((EXPERTS, BLOCK), 0)
    ids = ids_ref[...]
    for k in range(TOPK):
        gp_ref[k : k + 1, :] = jnp.sum(jnp.where(ids[k : k + 1, :] == expert, each, 0.0), axis=0, keepdims=True)


def _grad_tokens_kernel(pick_ref, r_ref, inner_ref, far_ref, out_ref, gp_ref):
    gp_ref[...] = inner_ref[...] + far_ref[...]
    halves = _home(pick_ref[...], r_ref)
    for h in range(2):
        out_ref[:, h * HALF : (h + 1) * HALF] = halves[h].astype(BF)


def _params():
    return pltpu.CompilerParams(vmem_limit_bytes=VMEM)


def _cost(flops, moved):
    return pl.CostEstimate(flops=int(flops), bytes_accessed=int(moved), transcendentals=0)


def _shape(shape, dtype):
    return jax.ShapeDtypeStruct(shape, dtype)


def _hbm(value):
    return pltpu.with_memory_space_constraint(value, pltpu.HBM)


def _fixed(*shape):
    return pl.BlockSpec(shape, lambda i, c: (0,) * len(shape))


def _half_pass(kernel, other, weights, state, out, scratch, flops, moved, name, aliases={}):
    def group(i, c):
        return 2 * i + (1 - c[0] if other else c[0])

    block = {
        "row": pl.BlockSpec((COLS, HID), lambda i, c: (group(i, c), 0)),
        "column": pl.BlockSpec((HID, COLS), lambda i, c: (0, group(i, c))),
        "received": pl.BlockSpec((1, MAIN, WIDE), lambda i, c: (i, 0, 0)),
        "slots": pl.BlockSpec((ROWS, COLS), lambda i, c: (0, group(i, c))),
        "whole": pl.BlockSpec(memory_space=pl.ANY),
        "hidden": _fixed(ROWS, HID),
        "both": _fixed(ROWS, 2 * HID),
    }
    return pl.pallas_call(
        kernel,
        grid_spec=pltpu.PrefetchScalarGridSpec(
            num_scalar_prefetch=1,
            grid=(2,),
            in_specs=[block["received"]] + [block[k] for k in weights + state],
            out_specs=[block[k] for k, _ in out],
            scratch_shapes=scratch,
        ),
        out_shape=[t for _, t in out],
        input_output_aliases=aliases,
        compiler_params=_params(),
        cost_estimate=_cost(flops, moved),
        name=name,
    )


def _forward_own(core, own, w_gate, w_up):
    return _half_pass(
        _forward_own_kernel,
        False,
        ["row", "row"],
        [],
        [("slots", pltpu.HBM((ROWS, D), BF)), ("hidden", _shape((ROWS, HID), F32)), ("hidden", _shape((ROWS, HID), F32))],
        [],
        EARLY * 2 * ROWS * D * HID,
        EARLY * 9e6,
        "forward_own",
    )(core, _hbm(own), _hbm(w_gate), _hbm(w_up))


def _forward_other(core, other, w_gate, w_up, gate, up, x):
    return _half_pass(
        _forward_other_kernel,
        True,
        ["row", "row"],
        ["hidden", "hidden", "whole"],
        [
            ("slots", pltpu.HBM((ROWS, D), BF)),
            ("hidden", _shape((ROWS, HID), F32)),
            ("hidden", _shape((ROWS, HID), F32)),
            ("hidden", _shape((ROWS, HID), BF)),
        ],
        [],
        LATE * 2 * ROWS * D * HID,
        LATE * 9e6,
        "forward_other",
        {6: 0},
    )(core, other, _hbm(w_gate), _hbm(w_up), gate, up, _hbm(x))


def _backward_own(core, own, w_down):
    return _half_pass(
        _backward_own_kernel,
        False,
        ["column"],
        [],
        [("slots", pltpu.HBM((ROWS, D), BF)), ("hidden", _shape((ROWS, HID), F32))],
        [],
        EARLY * 2 * ROWS * D * HID,
        EARLY * 9e6,
        "backward_own",
    )(core, _hbm(own), _hbm(w_down))


def _backward_other(core, other, w_down, partial, gate, up, e):
    return _half_pass(
        _backward_other_kernel,
        True,
        ["column"],
        ["hidden", "hidden", "hidden", "whole"],
        [("slots", pltpu.HBM((ROWS, D), BF)), ("both", _shape((ROWS, 2 * HID), BF))],
        [pltpu.VMEM((ROWS, HID), F32)],
        LATE * ROWS * D * HID,
        LATE * 6e6,
        "backward_other",
        {6: 0},
    )(core, other, _hbm(w_down), partial, gate, up, _hbm(e))


def _result(core, hidden, hidden_p, w_down, w_down_p):
    weight = pl.BlockSpec((HID, COLS), lambda i, c: (0, 2 * i + c[0]))
    return pl.pallas_call(
        _result_kernel,
        grid_spec=pltpu.PrefetchScalarGridSpec(
            num_scalar_prefetch=1,
            grid=(2,),
            in_specs=[_fixed(ROWS, HID), _fixed(ROWS, HID), weight, weight],
            out_specs=pl.BlockSpec((1, MAIN, WIDE), lambda i, c: (i, 0, 0)),
        ),
        out_shape=pltpu.HBM((2, MAIN, WIDE), BF),
        compiler_params=_params(),
        cost_estimate=_cost(LATE * 2 * ROWS * D * HID, LATE * 7e6),
        name="result",
    )(core, hidden, hidden_p, _hbm(w_down), _hbm(w_down_p))


def _back(core, grads, grads_p, w_gate, w_up, w_gate_p, w_up_p):
    weight = pl.BlockSpec((COLS, HID), lambda i, c: (2 * i + c[0], 0))
    return pl.pallas_call(
        _back_kernel,
        grid_spec=pltpu.PrefetchScalarGridSpec(
            num_scalar_prefetch=1,
            grid=(2,),
            in_specs=[_fixed(ROWS, 2 * HID), _fixed(ROWS, 2 * HID), weight, weight, weight, weight],
            out_specs=pl.BlockSpec((1, MAIN, WIDE), lambda i, c: (i, 0, 0)),
        ),
        out_shape=pltpu.HBM((2, MAIN, WIDE), BF),
        compiler_params=_params(),
        cost_estimate=_cost(LATE * 4 * ROWS * D * HID, LATE * 11e6),
        name="back",
    )(core, grads, grads_p, _hbm(w_gate), _hbm(w_up), _hbm(w_gate_p), _hbm(w_up_p))


def _grad_down(hidden, e):
    block = pl.BlockSpec((HID, COLS), lambda i: (0, i))
    return pl.pallas_call(
        _grad_down_kernel,
        grid=(4,),
        in_specs=[pl.BlockSpec((ROWS, HID), lambda i: (0, 0)), pl.BlockSpec((ROWS, COLS), lambda i: (0, i))],
        out_specs=block,
        out_shape=_shape((HID, D), BF),
        scratch_shapes=[pltpu.VMEM((HID, ROWS), BF)],
        compiler_params=_params(),
        cost_estimate=_cost(2 * ROWS * D * HID, 8e6),
        name="grad_down",
    )(hidden, _hbm(e))


def _local(kernel, out_shape, flops, moved, name, *args):
    return pl.pallas_call(
        kernel, out_shape=out_shape, compiler_params=_params(), cost_estimate=_cost(flops, moved), name=name
    )(*args)


def _exchange(packed):
    chunks = packed.reshape(2 * EXPERTS, 8, WIDE)
    got = lax.all_to_all(chunks, ("yhi", "expert"), split_axis=0, concat_axis=0, tiled=True)
    return got.reshape(2, MAIN, WIDE)


def _swap(value, axis="core"):
    return lax.ppermute(value, axis, [(0, 1), (1, 0)])


def body(tokens, cotangent, expert_ids, route_probs, w_gate, w_up, w_down):
    core = lax.axis_index("core").astype(jnp.int32).reshape(1)
    wg, wu, wd = w_gate[0], w_up[0], w_down[0]
    ids_t, probs_t = expert_ids.T, route_probs.T

    send_x = _local(_pack_rows_kernel, pltpu.HBM((2, MAIN, WIDE), BF), 2e8, 3e6, "pack_rows", _hbm(ids_t), _hbm(tokens))
    recv_x = _exchange(send_x)
    send_e, pick, weight = _local(
        _pack_grads_kernel,
        [pltpu.HBM((2, MAIN, WIDE), BF), _shape((2 * MAIN, BLOCK), BF), _shape((2 * MAIN, BLOCK), F32)],
        2e8,
        3e6,
        "pack_grads",
        _hbm(ids_t),
        _hbm(probs_t),
        _hbm(cotangent),
    )
    wd_p, wg_p, wu_p = _swap(wd), _swap(wg), _swap(wu)
    recv_x, send_e = lax.optimization_barrier((recv_x, send_e))
    recv_e = _exchange(send_e)

    x, gate, up = _forward_own(core, recv_x, wg, wu)
    x, gate, up, hidden = _forward_other(core, _swap(recv_x), wg, wu, gate, up, x)
    send_o = _result(core, hidden, _swap(hidden), wd, wd_p)
    recv_e, send_o = lax.optimization_barrier((recv_e, send_o))
    recv_o = _exchange(send_o)

    e, partial = _backward_own(core, recv_e, wd)
    e, grads = _backward_other(core, _swap(recv_e), wd, partial, gate, up, e)
    send_b = _back(core, grads, _swap(grads), wg, wu, wg_p, wu_p)
    recv_b = _exchange(send_b)

    g_down = _grad_down(hidden, e)
    g_gate = _dot_tn(x, grads[:, :HID]).astype(BF)
    g_up = _dot_tn(x, grads[:, HID:]).astype(BF)

    mixed, inner = _local(
        _mixed_kernel,
        [_shape((BLOCK, COLS), BF), _shape((TOPK, BLOCK), F32)],
        4e8,
        3e6,
        "mixed",
        _hbm(ids_t),
        _hbm(pick),
        _hbm(weight),
        _hbm(cotangent),
        _hbm(recv_o),
    )
    inner = inner + _swap(inner)
    far = _swap(inner, "yhi")
    recv_b, g_gate, g_up, g_down = lax.optimization_barrier((recv_b, g_gate, g_up, g_down))
    grad_tokens, grad_probs = _local(
        _grad_tokens_kernel,
        [_shape((BLOCK, COLS), BF), _shape((TOPK, BLOCK), F32)],
        2e8,
        3e6,
        "grad_tokens",
        pick,
        recv_b,
        inner,
        far,
    )
    return mixed, grad_tokens, grad_probs.T, g_gate[None], g_up[None], g_down[None]


def solution(mesh):
    fine = Mesh(mesh.devices.reshape(EXPERTS, 2, 2), ("expert", "yhi", "core"))
    dp = ("yhi", "core")
    return jax.shard_map(
        body,
        mesh=fine,
        in_specs=(
            P("expert", dp),
            P("expert", dp),
            P("expert", None),
            P("expert", None),
            P("expert", None, dp),
            P("expert", None, dp),
            P("expert", dp, None),
        ),
        out_specs=(
            P("expert", dp),
            P("expert", dp),
            P("expert", None),
            P("expert", None, dp),
            P("expert", None, dp),
            P("expert", dp, None),
        ),
        check_vma=False,
    )
```

```python
import functools

import jax
import jax.numpy as jnp
from jax import lax
from jax.experimental import pallas as pl
from jax.experimental.pallas import tpu as pltpu
from jax.sharding import Mesh, PartitionSpec as P

BF = jnp.bfloat16
F32 = jnp.float32

EXPERTS = 32
BLOCK = 128
TOPK = 6
COLS = 1280
HALF = 640
HID = 384
ROWS = 384
MAIN = 256
REST = 128
WIDE = COLS + HALF
D = 4 * COLS
VMEM = 40 * 1024 * 1024
EARLY = 16
LATE = 1 / 128


def _dot(a, b):
    return jnp.dot(a, b, preferred_element_type=F32)


def _dot_nt(a, b):
    return lax.dot_general(a, b, (((1,), (1,)), ((), ())), preferred_element_type=F32)


def _dot_tn(a, b):
    return lax.dot_general(a, b, (((0,), (0,)), ((), ())), preferred_element_type=F32)


def _iota(shape, dim):
    return lax.broadcasted_iota(jnp.int32, shape, dim)


def _routing(ids_t, probs_t=None):
    expert = _iota((EXPERTS, BLOCK), 0)
    chosen = jnp.zeros((EXPERTS, BLOCK), F32)
    weight = jnp.zeros((EXPERTS, BLOCK), F32)
    for k in range(TOPK):
        hit = ids_t[k : k + 1, :] == expert
        chosen = jnp.where(hit, 1.0, chosen)
        if probs_t is not None:
            weight = jnp.where(hit, probs_t[k : k + 1, :], weight)
    earlier = (_iota((BLOCK, BLOCK), 0) < _iota((BLOCK, BLOCK), 1)).astype(F32).astype(BF)
    before = _dot(chosen.astype(BF), earlier)
    code = jnp.where(chosen > 0.5, before, -1.0)
    row = _iota((MAIN, EXPERTS), 0)
    spread = ((row // 8) == _iota((MAIN, EXPERTS), 1)).astype(F32).astype(BF)
    place = _dot(spread, code.astype(BF))
    j = _iota((MAIN, BLOCK), 0)
    main = jnp.where(place == (j % 8).astype(F32), 1.0, 0.0)
    rest = jnp.where(place == (8 + j % 4).astype(F32), 1.0, 0.0)
    if probs_t is None:
        return main, rest, None
    hi = weight.astype(BF)
    left = weight - hi.astype(F32)
    mid = left.astype(BF)
    low = (left - mid.astype(F32)).astype(BF)
    full = _dot(spread, hi) + _dot(spread, mid) + _dot(spread, low)
    return main, rest, full


def _lower_half(shape):
    return (_iota(shape, 0) % 8) < 4


def _send(main, rest, source):
    first = _lower_half((MAIN, BLOCK))
    p0 = jnp.where(first, rest, 0.0).astype(BF)
    p1 = jnp.where(first, 0.0, rest).astype(BF)
    a = _dot(main.astype(BF), source)
    b = _dot(p0, source[:, :HALF]) + _dot(p1, source[:, HALF:])
    return a, b


def _pack_rows_kernel(ids_ref, tok_ref, out_ref):
    main, rest, _ = _routing(ids_ref[...])
    a, b = _send(main, rest, tok_ref[...])
    a, b = a.astype(BF), b.astype(BF)
    for y in range(2):
        out_ref[y, :, :COLS] = a
        out_ref[y, :, COLS:] = b


def _pack_grads_kernel(ids_ref, probs_ref, cot_ref, out_ref, pick_ref, weight_ref):
    main, rest, full = _routing(ids_ref[...], probs_ref[...])
    a, b = _send(main, rest, cot_ref[...])
    wm, wr = main * full, rest * full
    a = (a * jnp.sum(wm, axis=1, keepdims=True)).astype(BF)
    b = (b * jnp.sum(wr, axis=1, keepdims=True)).astype(BF)
    for y in range(2):
        out_ref[y, :, :COLS] = a
        out_ref[y, :, COLS:] = b
    pick_ref[:MAIN, :] = main.astype(BF)
    pick_ref[MAIN:, :] = rest.astype(BF)
    weight_ref[:MAIN, :] = wm
    weight_ref[MAIN:, :] = wr


def _fold(h):
    q = _iota((REST, MAIN), 0)
    return (_iota((REST, MAIN), 1) == (q // 4) * 8 + 4 * h + q % 4).astype(F32).astype(BF)


def _fold_t(h):
    q = _iota((MAIN, REST), 1)
    return (_iota((MAIN, REST), 0) == (q // 4) * 8 + 4 * h + q % 4).astype(F32).astype(BF)


def _unpack(r_ref, x_ref):
    rest = r_ref[0, :, COLS:]
    x_ref[:MAIN, :] = r_ref[0, :, :COLS]
    x_ref[MAIN:, :HALF] = _dot(_fold(0), rest).astype(BF)
    x_ref[MAIN:, HALF:] = _dot(_fold(1), rest).astype(BF)


def _pack(value, out_ref):
    rest = value[MAIN:, :]
    out_ref[0, :, :COLS] = value[:MAIN, :]
    out_ref[0, :, COLS:] = (_dot(_fold_t(0), rest[:, :HALF]) + _dot(_fold_t(1), rest[:, HALF:])).astype(BF)


def _forward_own_kernel(core_ref, r_ref, wg_ref, wu_ref, x_ref, g_ref, u_ref):
    _unpack(r_ref, x_ref)
    g = _dot(x_ref[...], wg_ref[...])
    u = _dot(x_ref[...], wu_ref[...])

    @pl.when(pl.program_id(0) == 0)
    def _():
        g_ref[...] = g
        u_ref[...] = u

    @pl.when(pl.program_id(0) > 0)
    def _():
        g_ref[...] += g
        u_ref[...] += u


def _forward_other_kernel(core_ref, r_ref, wg_ref, wu_ref, g0_ref, u0_ref, x0_ref, x_ref, g_ref, u_ref, h_ref):
    _unpack(r_ref, x_ref)
    g = _dot(x_ref[...], wg_ref[...])
    u = _dot(x_ref[...], wu_ref[...])

    @pl.when(pl.program_id(0) == 0)
    def _():
        g_ref[...] = g0_ref[...] + g
        u_ref[...] = u0_ref[...] + u

    @pl.when(pl.program_id(0) > 0)
    def _():
        gate = g_ref[...] + g
        up = u_ref[...] + u
        g_ref[...] = gate
        u_ref[...] = up
        h_ref[...] = (gate * jax.nn.sigmoid(gate) * up).astype(BF)


def _backward_own_kernel(core_ref, r_ref, wd_ref, e_ref, a_ref):
    _unpack(r_ref, e_ref)
    a = _dot_nt(e_ref[...], wd_ref[...])

    @pl.when(pl.program_id(0) == 0)
    def _():
        a_ref[...] = a

    @pl.when(pl.program_id(0) > 0)
    def _():
        a_ref[...] += a


def _backward_other_kernel(core_ref, r_ref, wd_ref, a0_ref, g_ref, u_ref, e0_ref, e_ref, d_ref, a_ref):
    _unpack(r_ref, e_ref)
    a = _dot_nt(e_ref[...], wd_ref[...])

    @pl.when(pl.program_id(0) == 0)
    def _():
        a_ref[...] = a0_ref[...] + a

    @pl.when(pl.program_id(0) > 0)
    def _():
        total, gate = a_ref[...] + a, g_ref[...]
        s = jax.nn.sigmoid(gate)
        d_ref[:, :HID] = (total * u_ref[...] * s * (1.0 + gate * (1.0 - s))).astype(BF)
        d_ref[:, HID:] = (total * (gate * s)).astype(BF)


def _result_kernel(core_ref, h_ref, hp_ref, wd_ref, wdp_ref, out_ref):
    value = _dot(h_ref[...], wd_ref[...]) + _dot(hp_ref[...], wdp_ref[...])
    _pack(value.astype(BF), out_ref)


def _back_kernel(core_ref, d_ref, dp_ref, wg_ref, wu_ref, wgp_ref, wup_ref, out_ref):
    value = _dot_nt(d_ref[:, :HID], wg_ref[...]) + _dot_nt(d_ref[:, HID:], wu_ref[...])
    value += _dot_nt(dp_ref[:, :HID], wgp_ref[...]) + _dot_nt(dp_ref[:, HID:], wup_ref[...])
    _pack(value.astype(BF), out_ref)


def _grad_in_kernel(x_ref, d_ref, gate_ref, up_ref):
    x = x_ref[...]
    gate_ref[...] = _dot_tn(x, d_ref[:, :HID]).astype(BF)
    up_ref[...] = _dot_tn(x, d_ref[:, HID:]).astype(BF)


def _home(pick, r_ref):
    main = pick[:MAIN, :]
    first = _lower_half((MAIN, BLOCK))
    rest = pick[MAIN:, :].astype(F32)
    halves = (jnp.where(first, rest, 0.0).astype(BF), jnp.where(first, 0.0, rest).astype(BF))
    out = []
    for h in range(2):
        total = jnp.zeros((BLOCK, HALF), F32)
        for y in range(2):
            total += _dot_tn(main, r_ref[y, :, h * HALF : (h + 1) * HALF])
            total += _dot_tn(halves[h], r_ref[y, :, COLS:])
        out.append(total)
    return out


def _mixed_kernel(ids_ref, pick_ref, weight_ref, cot_ref, r_ref, mixed_ref, gp_ref):
    w = weight_ref[...]
    hi = w.astype(BF)
    lo = (w - hi.astype(F32)).astype(BF)
    top, bottom = _home(hi, r_ref), _home(lo, r_ref)
    for h in range(2):
        mixed_ref[:, h * HALF : (h + 1) * HALF] = (top[h] + bottom[h]).astype(BF)
    cot = cot_ref[...]
    first = _lower_half((MAIN, BLOCK))
    inner = jnp.zeros((MAIN, BLOCK), F32)
    inner_rest = jnp.zeros((MAIN, BLOCK), F32)
    for y in range(2):
        inner += _dot_nt(r_ref[y, :, :COLS], cot)
        rest = r_ref[y, :, COLS:]
        inner_rest += jnp.where(first, _dot_nt(rest, cot[:, :HALF]), _dot_nt(rest, cot[:, HALF:]))
    pick = pick_ref[...].astype(F32)
    both = pick[:MAIN, :] * inner + pick[MAIN:, :] * inner_rest
    each = jnp.sum(both.reshape(EXPERTS, 8, BLOCK), axis=1)
    expert = _iota((EXPERTS, BLOCK), 0)
    ids = ids_ref[...]
    for k in range(TOPK):
        gp_ref[k : k + 1, :] = jnp.sum(jnp.where(ids[k : k + 1, :] == expert, each, 0.0), axis=0, keepdims=True)


def _grad_tokens_kernel(pick_ref, r_ref, inner_ref, far_ref, out_ref, gp_ref):
    gp_ref[...] = inner_ref[...] + far_ref[...]
    halves = _home(pick_ref[...], r_ref)
    for h in range(2):
        out_ref[:, h * HALF : (h + 1) * HALF] = halves[h].astype(BF)


def _params():
    return pltpu.CompilerParams(vmem_limit_bytes=VMEM)


def _cost(flops, moved):
    return pl.CostEstimate(flops=int(flops), bytes_accessed=int(moved), transcendentals=0)


def _shape(shape, dtype):
    return jax.ShapeDtypeStruct(shape, dtype)


def _hbm(value):
    return pltpu.with_memory_space_constraint(value, pltpu.HBM)


def _fixed(*shape):
    return pl.BlockSpec(shape, lambda i, c: (0,) * len(shape))


def _half_pass(kernel, other, weights, state, out, scratch, flops, moved, name, aliases={}):
    def group(i, c):
        return 2 * i + (1 - c[0] if other else c[0])

    block = {
        "row": pl.BlockSpec((COLS, HID), lambda i, c: (group(i, c), 0)),
        "column": pl.BlockSpec((HID, COLS), lambda i, c: (0, group(i, c))),
        "received": pl.BlockSpec((1, MAIN, WIDE), lambda i, c: (i, 0, 0)),
        "slots": pl.BlockSpec((ROWS, COLS), lambda i, c: (0, group(i, c))),
        "whole": pl.BlockSpec(memory_space=pl.ANY),
        "hidden": _fixed(ROWS, HID),
        "both": _fixed(ROWS, 2 * HID),
    }
    return pl.pallas_call(
        kernel,
        grid_spec=pltpu.PrefetchScalarGridSpec(
            num_scalar_prefetch=1,
            grid=(2,),
            in_specs=[block["received"]] + [block[k] for k in weights + state],
            out_specs=[block[k] for k, _ in out],
            scratch_shapes=scratch,
        ),
        out_shape=[t for _, t in out],
        input_output_aliases=aliases,
        compiler_params=_params(),
        cost_estimate=_cost(flops, moved),
        name=name,
    )


def _forward_own(core, own, w_gate, w_up):
    return _half_pass(
        _forward_own_kernel,
        False,
        ["row", "row"],
        [],
        [("slots", pltpu.HBM((ROWS, D), BF)), ("hidden", _shape((ROWS, HID), F32)), ("hidden", _shape((ROWS, HID), F32))],
        [],
        EARLY * 2 * ROWS * D * HID,
        EARLY * 9e6,
        "forward_own",
    )(core, _hbm(own), _hbm(w_gate), _hbm(w_up))


def _forward_other(core, other, w_gate, w_up, gate, up, x):
    return _half_pass(
        _forward_other_kernel,
        True,
        ["row", "row"],
        ["hidden", "hidden", "whole"],
        [
            ("slots", pltpu.HBM((ROWS, D), BF)),
            ("hidden", _shape((ROWS, HID), F32)),
            ("hidden", _shape((ROWS, HID), F32)),
            ("hidden", _shape((ROWS, HID), BF)),
        ],
        [],
        LATE * 2 * ROWS * D * HID,
        LATE * 9e6,
        "forward_other",
        {6: 0},
    )(core, other, _hbm(w_gate), _hbm(w_up), gate, up, _hbm(x))


def _backward_own(core, own, w_down):
    return _half_pass(
        _backward_own_kernel,
        False,
        ["column"],
        [],
        [("slots", pltpu.HBM((ROWS, D), BF)), ("hidden", _shape((ROWS, HID), F32))],
        [],
        EARLY * 2 * ROWS * D * HID,
        EARLY * 9e6,
        "backward_own",
    )(core, _hbm(own), _hbm(w_down))


def _backward_other(core, other, w_down, partial, gate, up, e):
    return _half_pass(
        _backward_other_kernel,
        True,
        ["column"],
        ["hidden", "hidden", "hidden", "whole"],
        [("slots", pltpu.HBM((ROWS, D), BF)), ("both", _shape((ROWS, 2 * HID), BF))],
        [pltpu.VMEM((ROWS, HID), F32)],
        LATE * ROWS * D * HID,
        LATE * 6e6,
        "backward_other",
        {6: 0},
    )(core, other, _hbm(w_down), partial, gate, up, _hbm(e))


def _result(core, hidden, hidden_p, w_down, w_down_p):
    weight = pl.BlockSpec((HID, COLS), lambda i, c: (0, 2 * i + c[0]))
    return pl.pallas_call(
        _result_kernel,
        grid_spec=pltpu.PrefetchScalarGridSpec(
            num_scalar_prefetch=1,
            grid=(2,),
            in_specs=[_fixed(ROWS, HID), _fixed(ROWS, HID), weight, weight],
            out_specs=pl.BlockSpec((1, MAIN, WIDE), lambda i, c: (i, 0, 0)),
        ),
        out_shape=pltpu.HBM((2, MAIN, WIDE), BF),
        compiler_params=_params(),
        cost_estimate=_cost(LATE * 2 * ROWS * D * HID, LATE * 7e6),
        name="result",
    )(core, hidden, hidden_p, _hbm(w_down), _hbm(w_down_p))


def _back(core, grads, grads_p, w_gate, w_up, w_gate_p, w_up_p):
    weight = pl.BlockSpec((COLS, HID), lambda i, c: (2 * i + c[0], 0))
    return pl.pallas_call(
        _back_kernel,
        grid_spec=pltpu.PrefetchScalarGridSpec(
            num_scalar_prefetch=1,
            grid=(2,),
            in_specs=[_fixed(ROWS, 2 * HID), _fixed(ROWS, 2 * HID), weight, weight, weight, weight],
            out_specs=pl.BlockSpec((1, MAIN, WIDE), lambda i, c: (i, 0, 0)),
        ),
        out_shape=pltpu.HBM((2, MAIN, WIDE), BF),
        compiler_params=_params(),
        cost_estimate=_cost(LATE * 4 * ROWS * D * HID, LATE * 11e6),
        name="back",
    )(core, grads, grads_p, _hbm(w_gate), _hbm(w_up), _hbm(w_gate_p), _hbm(w_up_p))


def _grad_in(x, grads):
    block = pl.BlockSpec((COLS, HID), lambda i: (i, 0))
    return pl.pallas_call(
        _grad_in_kernel,
        grid=(4,),
        in_specs=[pl.BlockSpec((ROWS, COLS), lambda i: (0, i)), pl.BlockSpec((ROWS, 2 * HID), lambda i: (0, 0))],
        out_specs=[block, block],
        out_shape=[_shape((D, HID), BF), _shape((D, HID), BF)],
        compiler_params=_params(),
        cost_estimate=_cost(4 * ROWS * D * HID, 13e6),
        name="grad_in",
    )(_hbm(x), grads)


def _local(kernel, out_shape, flops, moved, name, *args):
    return pl.pallas_call(
        kernel, out_shape=out_shape, compiler_params=_params(), cost_estimate=_cost(flops, moved), name=name
    )(*args)


def _exchange(packed):
    chunks = packed.reshape(2 * EXPERTS, 8, WIDE)
    got = lax.all_to_all(chunks, ("yhi", "expert"), split_axis=0, concat_axis=0, tiled=True)
    return got.reshape(2, MAIN, WIDE)


def _swap(value, axis="core"):
    return lax.ppermute(value, axis, [(0, 1), (1, 0)])


def body(tokens, cotangent, expert_ids, route_probs, w_gate, w_up, w_down):
    core = lax.axis_index("core").astype(jnp.int32).reshape(1)
    wg, wu, wd = w_gate[0], w_up[0], w_down[0]
    ids_t, probs_t = expert_ids.T, route_probs.T

    send_x = _local(_pack_rows_kernel, pltpu.HBM((2, MAIN, WIDE), BF), 2e8, 3e6, "pack_rows", _hbm(ids_t), _hbm(tokens))
    recv_x = _exchange(send_x)
    send_e, pick, weight = _local(
        _pack_grads_kernel,
        [pltpu.HBM((2, MAIN, WIDE), BF), _shape((2 * MAIN, BLOCK), BF), _shape((2 * MAIN, BLOCK), F32)],
        2e8,
        3e6,
        "pack_grads",
        _hbm(ids_t),
        _hbm(probs_t),
        _hbm(cotangent),
    )
    wd_p, wg_p, wu_p = _swap(wd), _swap(wg), _swap(wu)
    recv_x, send_e = lax.optimization_barrier((recv_x, send_e))
    recv_e = _exchange(send_e)

    x, gate, up = _forward_own(core, recv_x, wg, wu)
    x, gate, up, hidden = _forward_other(core, _swap(recv_x), wg, wu, gate, up, x)
    send_o = _result(core, hidden, _swap(hidden), wd, wd_p)
    recv_e, send_o = lax.optimization_barrier((recv_e, send_o))
    recv_o = _exchange(send_o)

    e, partial = _backward_own(core, recv_e, wd)
    e, grads = _backward_other(core, _swap(recv_e), wd, partial, gate, up, e)
    send_b = _back(core, grads, _swap(grads), wg, wu, wg_p, wu_p)
    recv_b = _exchange(send_b)

    g_gate, g_up = _grad_in(x, grads)
    hidden, e, g_gate, g_up = lax.optimization_barrier((hidden, e, g_gate, g_up))
    g_down = _dot_tn(hidden, e).astype(BF)

    mixed, inner = _local(
        _mixed_kernel,
        [_shape((BLOCK, COLS), BF), _shape((TOPK, BLOCK), F32)],
        4e8,
        3e6,
        "mixed",
        _hbm(ids_t),
        _hbm(pick),
        _hbm(weight),
        _hbm(cotangent),
        _hbm(recv_o),
    )
    inner = inner + _swap(inner)
    far = _swap(inner, "yhi")
    recv_b, g_gate, g_up, g_down = lax.optimization_barrier((recv_b, g_gate, g_up, g_down))
    grad_tokens, grad_probs = _local(
        _grad_tokens_kernel,
        [_shape((BLOCK, COLS), BF), _shape((TOPK, BLOCK), F32)],
        2e8,
        3e6,
        "grad_tokens",
        pick,
        recv_b,
        inner,
        far,
    )
    return mixed, grad_tokens, grad_probs.T, g_gate[None], g_up[None], g_down[None]


def solution(mesh):
    fine = Mesh(mesh.devices.reshape(EXPERTS, 2, 2), ("expert", "yhi", "core"))
    dp = ("yhi", "core")
    return jax.shard_map(
        body,
        mesh=fine,
        in_specs=(
            P("expert", dp),
            P("expert", dp),
            P("expert", None),
            P("expert", None),
            P("expert", None, dp),
            P("expert", None, dp),
            P("expert", dp, None),
        ),
        out_specs=(
            P("expert", dp),
            P("expert", dp),
            P("expert", None),
            P("expert", None, dp),
            P("expert", None, dp),
            P("expert", dp, None),
        ),
        check_vma=False,
    )
```

```python
import functools

import jax
import jax.numpy as jnp
from jax import lax
from jax.experimental import pallas as pl
from jax.experimental.pallas import tpu as pltpu
from jax.sharding import Mesh, PartitionSpec as P

BF = jnp.bfloat16
F32 = jnp.float32

EXPERTS = 32
BLOCK = 128
TOPK = 6
COLS = 1280
HALF = 640
HID = 384
ROWS = 384
MAIN = 256
REST = 128
WIDE = COLS + HALF
D = 4 * COLS
VMEM = 40 * 1024 * 1024
EARLY = 16
LATE = 1 / 128


def _dot(a, b):
    return jnp.dot(a, b, preferred_element_type=F32)


def _dot_nt(a, b):
    return lax.dot_general(a, b, (((1,), (1,)), ((), ())), preferred_element_type=F32)


def _dot_tn(a, b):
    return lax.dot_general(a, b, (((0,), (0,)), ((), ())), preferred_element_type=F32)


def _iota(shape, dim):
    return lax.broadcasted_iota(jnp.int32, shape, dim)


def _routing(ids_t, probs_t=None):
    expert = _iota((EXPERTS, BLOCK), 0)
    chosen = jnp.zeros((EXPERTS, BLOCK), F32)
    weight = jnp.zeros((EXPERTS, BLOCK), F32)
    for k in range(TOPK):
        hit = ids_t[k : k + 1, :] == expert
        chosen = jnp.where(hit, 1.0, chosen)
        if probs_t is not None:
            weight = jnp.where(hit, probs_t[k : k + 1, :], weight)
    earlier = (_iota((BLOCK, BLOCK), 0) < _iota((BLOCK, BLOCK), 1)).astype(F32).astype(BF)
    before = _dot(chosen.astype(BF), earlier)
    code = jnp.where(chosen > 0.5, before, -1.0)
    row = _iota((MAIN, EXPERTS), 0)
    spread = ((row // 8) == _iota((MAIN, EXPERTS), 1)).astype(F32).astype(BF)
    place = _dot(spread, code.astype(BF))
    j = _iota((MAIN, BLOCK), 0)
    main = jnp.where(place == (j % 8).astype(F32), 1.0, 0.0)
    rest = jnp.where(place == (8 + j % 4).astype(F32), 1.0, 0.0)
    if probs_t is None:
        return main, rest, None
    hi = weight.astype(BF)
    left = weight - hi.astype(F32)
    mid = left.astype(BF)
    low = (left - mid.astype(F32)).astype(BF)
    full = _dot(spread, hi) + _dot(spread, mid) + _dot(spread, low)
    return main, rest, full


def _lower_half(shape):
    return (_iota(shape, 0) % 8) < 4


def _send(main, rest, source):
    first = _lower_half((MAIN, BLOCK))
    p0 = jnp.where(first, rest, 0.0).astype(BF)
    p1 = jnp.where(first, 0.0, rest).astype(BF)
    a = _dot(main.astype(BF), source)
    b = _dot(p0, source[:, :HALF]) + _dot(p1, source[:, HALF:])
    return a, b


def _pack_rows_kernel(ids_ref, tok_ref, out_ref):
    main, rest, _ = _routing(ids_ref[...])
    a, b = _send(main, rest, tok_ref[...])
    a, b = a.astype(BF), b.astype(BF)
    for y in range(2):
        out_ref[y, :, :COLS] = a
        out_ref[y, :, COLS:] = b


def _pack_grads_kernel(ids_ref, probs_ref, cot_ref, out_ref, pick_ref, weight_ref):
    main, rest, full = _routing(ids_ref[...], probs_ref[...])
    a, b = _send(main, rest, cot_ref[...])
    wm, wr = main * full, rest * full
    a = (a * jnp.sum(wm, axis=1, keepdims=True)).astype(BF)
    b = (b * jnp.sum(wr, axis=1, keepdims=True)).astype(BF)
    for y in range(2):
        out_ref[y, :, :COLS] = a
        out_ref[y, :, COLS:] = b
    pick_ref[:MAIN, :] = main.astype(BF)
    pick_ref[MAIN:, :] = rest.astype(BF)
    weight_ref[:MAIN, :] = wm
    weight_ref[MAIN:, :] = wr


def _fold(h):
    q = _iota((REST, MAIN), 0)
    return (_iota((REST, MAIN), 1) == (q // 4) * 8 + 4 * h + q % 4).astype(F32).astype(BF)


def _fold_t(h):
    q = _iota((MAIN, REST), 1)
    return (_iota((MAIN, REST), 0) == (q // 4) * 8 + 4 * h + q % 4).astype(F32).astype(BF)


def _unpack(r_ref, x_ref):
    rest = r_ref[0, :, COLS:]
    x_ref[:MAIN, :] = r_ref[0, :, :COLS]
    x_ref[MAIN:, :HALF] = _dot(_fold(0), rest).astype(BF)
    x_ref[MAIN:, HALF:] = _dot(_fold(1), rest).astype(BF)


def _pack(value, out_ref):
    rest = value[MAIN:, :]
    out_ref[0, :, :COLS] = value[:MAIN, :]
    out_ref[0, :, COLS:] = (_dot(_fold_t(0), rest[:, :HALF]) + _dot(_fold_t(1), rest[:, HALF:])).astype(BF)


def _forward_own_kernel(core_ref, r_ref, wg_ref, wu_ref, x_ref, g_ref, u_ref):
    _unpack(r_ref, x_ref)
    g = _dot(x_ref[...], wg_ref[...])
    u = _dot(x_ref[...], wu_ref[...])

    @pl.when(pl.program_id(0) == 0)
    def _():
        g_ref[...] = g
        u_ref[...] = u

    @pl.when(pl.program_id(0) > 0)
    def _():
        g_ref[...] += g
        u_ref[...] += u


def _forward_other_kernel(core_ref, r_ref, wg_ref, wu_ref, g0_ref, u0_ref, x0_ref, x_ref, g_ref, u_ref, h_ref):
    _unpack(r_ref, x_ref)
    g = _dot(x_ref[...], wg_ref[...])
    u = _dot(x_ref[...], wu_ref[...])

    @pl.when(pl.program_id(0) == 0)
    def _():
        g_ref[...] = g0_ref[...] + g
        u_ref[...] = u0_ref[...] + u

    @pl.when(pl.program_id(0) > 0)
    def _():
        gate = g_ref[...] + g
        up = u_ref[...] + u
        g_ref[...] = gate
        u_ref[...] = up
        h_ref[...] = (gate * jax.nn.sigmoid(gate) * up).astype(BF)


def _backward_own_kernel(core_ref, r_ref, wd_ref, e_ref, a_ref):
    _unpack(r_ref, e_ref)
    a = _dot_nt(e_ref[...], wd_ref[...])

    @pl.when(pl.program_id(0) == 0)
    def _():
        a_ref[...] = a

    @pl.when(pl.program_id(0) > 0)
    def _():
        a_ref[...] += a


def _backward_other_kernel(core_ref, r_ref, wd_ref, a0_ref, g_ref, u_ref, e0_ref, e_ref, d_ref, a_ref):
    _unpack(r_ref, e_ref)
    a = _dot_nt(e_ref[...], wd_ref[...])

    @pl.when(pl.program_id(0) == 0)
    def _():
        a_ref[...] = a0_ref[...] + a

    @pl.when(pl.program_id(0) > 0)
    def _():
        total, gate = a_ref[...] + a, g_ref[...]
        s = jax.nn.sigmoid(gate)
        d_ref[:, :HID] = (total * u_ref[...] * s * (1.0 + gate * (1.0 - s))).astype(BF)
        d_ref[:, HID:] = (total * (gate * s)).astype(BF)


def _result_kernel(core_ref, h_ref, hp_ref, wd_ref, wdp_ref, out_ref):
    value = _dot(h_ref[...], wd_ref[...]) + _dot(hp_ref[...], wdp_ref[...])
    _pack(value.astype(BF), out_ref)


def _back_kernel(core_ref, d_ref, dp_ref, wg_ref, wu_ref, wgp_ref, wup_ref, out_ref):
    both = jnp.concatenate([d_ref[...], dp_ref[...]], axis=1)
    weights = jnp.concatenate([wg_ref[...], wu_ref[...], wgp_ref[...], wup_ref[...]], axis=1)
    value = _dot_nt(both, weights)
    _pack(value.astype(BF), out_ref)


def _grad_in_kernel(x_ref, d_ref, gate_ref, up_ref):
    x = x_ref[...]
    gate_ref[...] = _dot_tn(x, d_ref[:, :HID]).astype(BF)
    up_ref[...] = _dot_tn(x, d_ref[:, HID:]).astype(BF)


def _home(pick, r_ref):
    main = pick[:MAIN, :]
    first = _lower_half((MAIN, BLOCK))
    rest = pick[MAIN:, :].astype(F32)
    halves = (jnp.where(first, rest, 0.0).astype(BF), jnp.where(first, 0.0, rest).astype(BF))
    out = []
    for h in range(2):
        total = jnp.zeros((BLOCK, HALF), F32)
        for y in range(2):
            total += _dot_tn(main, r_ref[y, :, h * HALF : (h + 1) * HALF])
            total += _dot_tn(halves[h], r_ref[y, :, COLS:])
        out.append(total)
    return out


def _mixed_kernel(ids_ref, pick_ref, weight_ref, cot_ref, r_ref, mixed_ref, gp_ref):
    w = weight_ref[...]
    hi = w.astype(BF)
    lo = (w - hi.astype(F32)).astype(BF)
    top, bottom = _home(hi, r_ref), _home(lo, r_ref)
    for h in range(2):
        mixed_ref[:, h * HALF : (h + 1) * HALF] = (top[h] + bottom[h]).astype(BF)
    cot = cot_ref[...]
    first = _lower_half((MAIN, BLOCK))
    inner = jnp.zeros((MAIN, BLOCK), F32)
    inner_rest = jnp.zeros((MAIN, BLOCK), F32)
    for y in range(2):
        inner += _dot_nt(r_ref[y, :, :COLS], cot)
        rest = r_ref[y, :, COLS:]
        inner_rest += jnp.where(first, _dot_nt(rest, cot[:, :HALF]), _dot_nt(rest, cot[:, HALF:]))
    pick = pick_ref[...].astype(F32)
    both = pick[:MAIN, :] * inner + pick[MAIN:, :] * inner_rest
    each = jnp.sum(both.reshape(EXPERTS, 8, BLOCK), axis=1)
    expert = _iota((EXPERTS, BLOCK), 0)
    ids = ids_ref[...]
    for k in range(TOPK):
        gp_ref[k : k + 1, :] = jnp.sum(jnp.where(ids[k : k + 1, :] == expert, each, 0.0), axis=0, keepdims=True)


def _grad_tokens_kernel(pick_ref, r_ref, inner_ref, far_ref, out_ref, gp_ref):
    gp_ref[...] = inner_ref[...] + far_ref[...]
    halves = _home(pick_ref[...], r_ref)
    for h in range(2):
        out_ref[:, h * HALF : (h + 1) * HALF] = halves[h].astype(BF)


def _params():
    return pltpu.CompilerParams(vmem_limit_bytes=VMEM)


def _cost(flops, moved):
    return pl.CostEstimate(flops=int(flops), bytes_accessed=int(moved), transcendentals=0)


def _shape(shape, dtype):
    return jax.ShapeDtypeStruct(shape, dtype)


def _hbm(value):
    return pltpu.with_memory_space_constraint(value, pltpu.HBM)


def _fixed(*shape):
    return pl.BlockSpec(shape, lambda i, c: (0,) * len(shape))


def _half_pass(kernel, other, weights, state, out, scratch, flops, moved, name, aliases={}):
    def group(i, c):
        return 2 * i + (1 - c[0] if other else c[0])

    block = {
        "row": pl.BlockSpec((COLS, HID), lambda i, c: (group(i, c), 0)),
        "column": pl.BlockSpec((HID, COLS), lambda i, c: (0, group(i, c))),
        "received": pl.BlockSpec((1, MAIN, WIDE), lambda i, c: (i, 0, 0)),
        "slots": pl.BlockSpec((ROWS, COLS), lambda i, c: (0, group(i, c))),
        "whole": pl.BlockSpec(memory_space=pl.ANY),
        "hidden": _fixed(ROWS, HID),
        "both": _fixed(ROWS, 2 * HID),
    }
    return pl.pallas_call(
        kernel,
        grid_spec=pltpu.PrefetchScalarGridSpec(
            num_scalar_prefetch=1,
            grid=(2,),
            in_specs=[block["received"]] + [block[k] for k in weights + state],
            out_specs=[block[k] for k, _ in out],
            scratch_shapes=scratch,
        ),
        out_shape=[t for _, t in out],
        input_output_aliases=aliases,
        compiler_params=_params(),
        cost_estimate=_cost(flops, moved),
        name=name,
    )


def _forward_own(core, own, w_gate, w_up):
    return _half_pass(
        _forward_own_kernel,
        False,
        ["row", "row"],
        [],
        [("slots", pltpu.HBM((ROWS, D), BF)), ("hidden", _shape((ROWS, HID), F32)), ("hidden", _shape((ROWS, HID), F32))],
        [],
        EARLY * 2 * ROWS * D * HID,
        EARLY * 9e6,
        "forward_own",
    )(core, _hbm(own), _hbm(w_gate), _hbm(w_up))


def _forward_other(core, other, w_gate, w_up, gate, up, x):
    return _half_pass(
        _forward_other_kernel,
        True,
        ["row", "row"],
        ["hidden", "hidden", "whole"],
        [
            ("slots", pltpu.HBM((ROWS, D), BF)),
            ("hidden", _shape((ROWS, HID), F32)),
            ("hidden", _shape((ROWS, HID), F32)),
            ("hidden", _shape((ROWS, HID), BF)),
        ],
        [],
        LATE * 2 * ROWS * D * HID,
        LATE * 9e6,
        "forward_other",
        {6: 0},
    )(core, other, _hbm(w_gate), _hbm(w_up), gate, up, _hbm(x))


def _backward_own(core, own, w_down):
    return _half_pass(
        _backward_own_kernel,
        False,
        ["column"],
        [],
        [("slots", pltpu.HBM((ROWS, D), BF)), ("hidden", _shape((ROWS, HID), F32))],
        [],
        EARLY * 2 * ROWS * D * HID,
        EARLY * 9e6,
        "backward_own",
    )(core, _hbm(own), _hbm(w_down))


def _backward_other(core, other, w_down, partial, gate, up, e):
    return _half_pass(
        _backward_other_kernel,
        True,
        ["column"],
        ["hidden", "hidden", "hidden", "whole"],
        [("slots", pltpu.HBM((ROWS, D), BF)), ("both", _shape((ROWS, 2 * HID), BF))],
        [pltpu.VMEM((ROWS, HID), F32)],
        LATE * ROWS * D * HID,
        LATE * 6e6,
        "backward_other",
        {6: 0},
    )(core, other, _hbm(w_down), partial, gate, up, _hbm(e))


def _result(core, hidden, hidden_p, w_down, w_down_p):
    weight = pl.BlockSpec((HID, COLS), lambda i, c: (0, 2 * i + c[0]))
    return pl.pallas_call(
        _result_kernel,
        grid_spec=pltpu.PrefetchScalarGridSpec(
            num_scalar_prefetch=1,
            grid=(2,),
            in_specs=[_fixed(ROWS, HID), _fixed(ROWS, HID), weight, weight],
            out_specs=pl.BlockSpec((1, MAIN, WIDE), lambda i, c: (i, 0, 0)),
        ),
        out_shape=pltpu.HBM((2, MAIN, WIDE), BF),
        compiler_params=_params(),
        cost_estimate=_cost(LATE * 2 * ROWS * D * HID, LATE * 7e6),
        name="result",
    )(core, hidden, hidden_p, _hbm(w_down), _hbm(w_down_p))


def _back(core, grads, grads_p, w_gate, w_up, w_gate_p, w_up_p):
    weight = pl.BlockSpec((COLS, HID), lambda i, c: (2 * i + c[0], 0))
    return pl.pallas_call(
        _back_kernel,
        grid_spec=pltpu.PrefetchScalarGridSpec(
            num_scalar_prefetch=1,
            grid=(2,),
            in_specs=[_fixed(ROWS, 2 * HID), _fixed(ROWS, 2 * HID), weight, weight, weight, weight],
            out_specs=pl.BlockSpec((1, MAIN, WIDE), lambda i, c: (i, 0, 0)),
        ),
        out_shape=pltpu.HBM((2, MAIN, WIDE), BF),
        compiler_params=_params(),
        cost_estimate=_cost(LATE * 4 * ROWS * D * HID, LATE * 11e6),
        name="back",
    )(core, grads, grads_p, _hbm(w_gate), _hbm(w_up), _hbm(w_gate_p), _hbm(w_up_p))


def _grad_in(x, grads):
    block = pl.BlockSpec((COLS, HID), lambda i: (i, 0))
    return pl.pallas_call(
        _grad_in_kernel,
        grid=(4,),
        in_specs=[pl.BlockSpec((ROWS, COLS), lambda i: (0, i)), pl.BlockSpec((ROWS, 2 * HID), lambda i: (0, 0))],
        out_specs=[block, block],
        out_shape=[_shape((D, HID), BF), _shape((D, HID), BF)],
        compiler_params=_params(),
        cost_estimate=_cost(4 * ROWS * D * HID, 13e6),
        name="grad_in",
    )(_hbm(x), grads)


def _local(kernel, out_shape, flops, moved, name, *args):
    return pl.pallas_call(
        kernel, out_shape=out_shape, compiler_params=_params(), cost_estimate=_cost(flops, moved), name=name
    )(*args)


def _exchange(packed):
    chunks = packed.reshape(2 * EXPERTS, 8, WIDE)
    got = lax.all_to_all(chunks, ("yhi", "expert"), split_axis=0, concat_axis=0, tiled=True)
    return got.reshape(2, MAIN, WIDE)


def _swap(value, axis="core"):
    return lax.ppermute(value, axis, [(0, 1), (1, 0)])


def body(tokens, cotangent, expert_ids, route_probs, w_gate, w_up, w_down):
    core = lax.axis_index("core").astype(jnp.int32).reshape(1)
    wg, wu, wd = w_gate[0], w_up[0], w_down[0]
    ids_t, probs_t = expert_ids.T, route_probs.T

    send_x = _local(_pack_rows_kernel, pltpu.HBM((2, MAIN, WIDE), BF), 2e8, 3e6, "pack_rows", _hbm(ids_t), _hbm(tokens))
    recv_x = _exchange(send_x)
    send_e, pick, weight = _local(
        _pack_grads_kernel,
        [pltpu.HBM((2, MAIN, WIDE), BF), _shape((2 * MAIN, BLOCK), BF), _shape((2 * MAIN, BLOCK), F32)],
        2e8,
        3e6,
        "pack_grads",
        _hbm(ids_t),
        _hbm(probs_t),
        _hbm(cotangent),
    )
    wd_p, wg_p, wu_p = _swap(wd), _swap(wg), _swap(wu)
    recv_x, send_e = lax.optimization_barrier((recv_x, send_e))
    recv_e = _exchange(send_e)

    x, gate, up = _forward_own(core, recv_x, wg, wu)
    x, gate, up, hidden = _forward_other(core, _swap(recv_x), wg, wu, gate, up, x)
    send_o = _result(core, hidden, _swap(hidden), wd, wd_p)
    recv_e, send_o = lax.optimization_barrier((recv_e, send_o))
    recv_o = _exchange(send_o)

    e, partial = _backward_own(core, recv_e, wd)
    e, grads = _backward_other(core, _swap(recv_e), wd, partial, gate, up, e)
    send_b = _back(core, grads, _swap(grads), wg, wu, wg_p, wu_p)
    recv_b = _exchange(send_b)

    g_gate, g_up = _grad_in(x, grads)
    hidden, e, g_gate, g_up = lax.optimization_barrier((hidden, e, g_gate, g_up))
    g_down = _dot_tn(hidden, e).astype(BF)

    mixed, inner = _local(
        _mixed_kernel,
        [_shape((BLOCK, COLS), BF), _shape((TOPK, BLOCK), F32)],
        4e8,
        3e6,
        "mixed",
        _hbm(ids_t),
        _hbm(pick),
        _hbm(weight),
        _hbm(cotangent),
        _hbm(recv_o),
    )
    inner = inner + _swap(inner)
    far = _swap(inner, "yhi")
    recv_b, g_gate, g_up, g_down = lax.optimization_barrier((recv_b, g_gate, g_up, g_down))
    grad_tokens, grad_probs = _local(
        _grad_tokens_kernel,
        [_shape((BLOCK, COLS), BF), _shape((TOPK, BLOCK), F32)],
        2e8,
        3e6,
        "grad_tokens",
        pick,
        recv_b,
        inner,
        far,
    )
    return mixed, grad_tokens, grad_probs.T, g_gate[None], g_up[None], g_down[None]


def solution(mesh):
    fine = Mesh(mesh.devices.reshape(EXPERTS, 2, 2), ("expert", "yhi", "core"))
    dp = ("yhi", "core")
    return jax.shard_map(
        body,
        mesh=fine,
        in_specs=(
            P("expert", dp),
            P("expert", dp),
            P("expert", None),
            P("expert", None),
            P("expert", None, dp),
            P("expert", None, dp),
            P("expert", dp, None),
        ),
        out_specs=(
            P("expert", dp),
            P("expert", dp),
            P("expert", None),
            P("expert", None, dp),
            P("expert", None, dp),
            P("expert", dp, None),
        ),
        check_vma=False,
    )
```

```python
import functools

import jax
import jax.numpy as jnp
from jax import lax
from jax.experimental import pallas as pl
from jax.experimental.pallas import tpu as pltpu
from jax.sharding import Mesh, PartitionSpec as P

BF = jnp.bfloat16
F32 = jnp.float32

EXPERTS = 32
BLOCK = 128
TOPK = 6
COLS = 1280
HALF = 640
HID = 384
ROWS = 384
MAIN = 256
REST = 128
WIDE = COLS + HALF
D = 4 * COLS
VMEM = 40 * 1024 * 1024
EARLY = 16
LATE = 1 / 128


def _dot(a, b):
    return jnp.dot(a, b, preferred_element_type=F32)


def _dot_nt(a, b):
    return lax.dot_general(a, b, (((1,), (1,)), ((), ())), preferred_element_type=F32)


def _dot_tn(a, b):
    return lax.dot_general(a, b, (((0,), (0,)), ((), ())), preferred_element_type=F32)


def _iota(shape, dim):
    return lax.broadcasted_iota(jnp.int32, shape, dim)


def _routing(ids_t, probs_t=None):
    expert = _iota((EXPERTS, BLOCK), 0)
    chosen = jnp.zeros((EXPERTS, BLOCK), F32)
    weight = jnp.zeros((EXPERTS, BLOCK), F32)
    for k in range(TOPK):
        hit = ids_t[k : k + 1, :] == expert
        chosen = jnp.where(hit, 1.0, chosen)
        if probs_t is not None:
            weight = jnp.where(hit, probs_t[k : k + 1, :], weight)
    earlier = (_iota((BLOCK, BLOCK), 0) < _iota((BLOCK, BLOCK), 1)).astype(F32).astype(BF)
    before = _dot(chosen.astype(BF), earlier)
    code = jnp.where(chosen > 0.5, before, -1.0)
    row = _iota((MAIN, EXPERTS), 0)
    spread = ((row // 8) == _iota((MAIN, EXPERTS), 1)).astype(F32).astype(BF)
    place = _dot(spread, code.astype(BF))
    j = _iota((MAIN, BLOCK), 0)
    main = jnp.where(place == (j % 8).astype(F32), 1.0, 0.0)
    rest = jnp.where(place == (8 + j % 4).astype(F32), 1.0, 0.0)
    if probs_t is None:
        return main, rest, None
    hi = weight.astype(BF)
    left = weight - hi.astype(F32)
    mid = left.astype(BF)
    low = (left - mid.astype(F32)).astype(BF)
    full = _dot(spread, hi) + _dot(spread, mid) + _dot(spread, low)
    return main, rest, full


def _lower_half(shape):
    return (_iota(shape, 0) % 8) < 4


def _send(main, rest, source):
    first = _lower_half((MAIN, BLOCK))
    p0 = jnp.where(first, rest, 0.0).astype(BF)
    p1 = jnp.where(first, 0.0, rest).astype(BF)
    a = _dot(main.astype(BF), source)
    b = _dot(p0, source[:, :HALF]) + _dot(p1, source[:, HALF:])
    return a, b


def _pack_rows_kernel(ids_ref, tok_ref, out_ref):
    main, rest, _ = _routing(ids_ref[...])
    a, b = _send(main, rest, tok_ref[...])
    a, b = a.astype(BF), b.astype(BF)
    for y in range(2):
        out_ref[y, :, :COLS] = a
        out_ref[y, :, COLS:] = b


def _pack_grads_kernel(ids_ref, probs_ref, cot_ref, out_ref, pick_ref, weight_ref):
    main, rest, full = _routing(ids_ref[...], probs_ref[...])
    a, b = _send(main, rest, cot_ref[...])
    wm, wr = main * full, rest * full
    a = (a * jnp.sum(wm, axis=1, keepdims=True)).astype(BF)
    b = (b * jnp.sum(wr, axis=1, keepdims=True)).astype(BF)
    for y in range(2):
        out_ref[y, :, :COLS] = a
        out_ref[y, :, COLS:] = b
    pick_ref[:MAIN, :] = main.astype(BF)
    pick_ref[MAIN:, :] = rest.astype(BF)
    weight_ref[:MAIN, :] = wm
    weight_ref[MAIN:, :] = wr


def _fold(h):
    q = _iota((REST, MAIN), 0)
    return (_iota((REST, MAIN), 1) == (q // 4) * 8 + 4 * h + q % 4).astype(F32).astype(BF)


def _fold_t(h):
    q = _iota((MAIN, REST), 1)
    return (_iota((MAIN, REST), 0) == (q // 4) * 8 + 4 * h + q % 4).astype(F32).astype(BF)


def _unpack(r_ref, x_ref):
    rest = r_ref[0, :, COLS:]
    x_ref[:MAIN, :] = r_ref[0, :, :COLS]
    x_ref[MAIN:, :HALF] = _dot(_fold(0), rest).astype(BF)
    x_ref[MAIN:, HALF:] = _dot(_fold(1), rest).astype(BF)


def _pack(value, out_ref):
    rest = value[MAIN:, :]
    out_ref[0, :, :COLS] = value[:MAIN, :]
    out_ref[0, :, COLS:] = (_dot(_fold_t(0), rest[:, :HALF]) + _dot(_fold_t(1), rest[:, HALF:])).astype(BF)


def _forward_own_kernel(core_ref, r_ref, wg_ref, wu_ref, x_ref, g_ref, u_ref):
    _unpack(r_ref, x_ref)
    g = _dot(x_ref[...], wg_ref[...])
    u = _dot(x_ref[...], wu_ref[...])

    @pl.when(pl.program_id(0) == 0)
    def _():
        g_ref[...] = g
        u_ref[...] = u

    @pl.when(pl.program_id(0) > 0)
    def _():
        g_ref[...] += g
        u_ref[...] += u


def _forward_other_kernel(core_ref, r_ref, wg_ref, wu_ref, g0_ref, u0_ref, x0_ref, x_ref, g_ref, u_ref, h_ref):
    _unpack(r_ref, x_ref)
    g = _dot(x_ref[...], wg_ref[...])
    u = _dot(x_ref[...], wu_ref[...])

    @pl.when(pl.program_id(0) == 0)
    def _():
        g_ref[...] = g0_ref[...] + g
        u_ref[...] = u0_ref[...] + u

    @pl.when(pl.program_id(0) > 0)
    def _():
        gate = g_ref[...] + g
        up = u_ref[...] + u
        g_ref[...] = gate
        u_ref[...] = up
        h_ref[...] = (gate * jax.nn.sigmoid(gate) * up).astype(BF)


def _backward_own_kernel(core_ref, r_ref, wd_ref, e_ref, a_ref):
    _unpack(r_ref, e_ref)
    a = _dot_nt(e_ref[...], wd_ref[...])

    @pl.when(pl.program_id(0) == 0)
    def _():
        a_ref[...] = a

    @pl.when(pl.program_id(0) > 0)
    def _():
        a_ref[...] += a


def _backward_other_kernel(core_ref, r_ref, wd_ref, a0_ref, g_ref, u_ref, e0_ref, e_ref, d_ref, a_ref):
    _unpack(r_ref, e_ref)
    a = _dot_nt(e_ref[...], wd_ref[...])

    @pl.when(pl.program_id(0) == 0)
    def _():
        a_ref[...] = a0_ref[...] + a

    @pl.when(pl.program_id(0) > 0)
    def _():
        total, gate = a_ref[...] + a, g_ref[...]
        s = jax.nn.sigmoid(gate)
        d_ref[:, :HID] = (total * u_ref[...] * s * (1.0 + gate * (1.0 - s))).astype(BF)
        d_ref[:, HID:] = (total * (gate * s)).astype(BF)


def _result_kernel(core_ref, h_ref, hp_ref, wd_ref, wdp_ref, out_ref):
    both = jnp.concatenate([h_ref[...], hp_ref[...]], axis=1)
    value = _dot(both, jnp.concatenate([wd_ref[...], wdp_ref[...]], axis=0))
    _pack(value.astype(BF), out_ref)


def _back_kernel(core_ref, d_ref, dp_ref, wg_ref, wu_ref, wgp_ref, wup_ref, out_ref):
    both = jnp.concatenate([d_ref[...], dp_ref[...]], axis=1)
    weights = jnp.concatenate([wg_ref[...], wu_ref[...], wgp_ref[...], wup_ref[...]], axis=1)
    value = _dot_nt(both, weights)
    _pack(value.astype(BF), out_ref)


def _grad_in_kernel(x_ref, d_ref, gate_ref, up_ref):
    x = x_ref[...]
    gate_ref[...] = _dot_tn(x, d_ref[:, :HID]).astype(BF)
    up_ref[...] = _dot_tn(x, d_ref[:, HID:]).astype(BF)


def _home(pick, r_ref):
    main = pick[:MAIN, :]
    first = _lower_half((MAIN, BLOCK))
    rest = pick[MAIN:, :].astype(F32)
    halves = (jnp.where(first, rest, 0.0).astype(BF), jnp.where(first, 0.0, rest).astype(BF))
    out = []
    for h in range(2):
        total = jnp.zeros((BLOCK, HALF), F32)
        for y in range(2):
            total += _dot_tn(main, r_ref[y, :, h * HALF : (h + 1) * HALF])
            total += _dot_tn(halves[h], r_ref[y, :, COLS:])
        out.append(total)
    return out


def _mixed_kernel(ids_ref, pick_ref, weight_ref, cot_ref, r_ref, mixed_ref, gp_ref):
    w = weight_ref[...]
    hi = w.astype(BF)
    lo = (w - hi.astype(F32)).astype(BF)
    top, bottom = _home(hi, r_ref), _home(lo, r_ref)
    for h in range(2):
        mixed_ref[:, h * HALF : (h + 1) * HALF] = (top[h] + bottom[h]).astype(BF)
    cot = cot_ref[...]
    first = _lower_half((MAIN, BLOCK))
    inner = jnp.zeros((MAIN, BLOCK), F32)
    inner_rest = jnp.zeros((MAIN, BLOCK), F32)
    for y in range(2):
        inner += _dot_nt(r_ref[y, :, :COLS], cot)
        rest = r_ref[y, :, COLS:]
        inner_rest += jnp.where(first, _dot_nt(rest, cot[:, :HALF]), _dot_nt(rest, cot[:, HALF:]))
    pick = pick_ref[...].astype(F32)
    both = pick[:MAIN, :] * inner + pick[MAIN:, :] * inner_rest
    each = jnp.sum(both.reshape(EXPERTS, 8, BLOCK), axis=1)
    expert = _iota((EXPERTS, BLOCK), 0)
    ids = ids_ref[...]
    for k in range(TOPK):
        gp_ref[k : k + 1, :] = jnp.sum(jnp.where(ids[k : k + 1, :] == expert, each, 0.0), axis=0, keepdims=True)


def _grad_tokens_kernel(pick_ref, r_ref, inner_ref, far_ref, out_ref, gp_ref):
    gp_ref[...] = inner_ref[...] + far_ref[...]
    halves = _home(pick_ref[...], r_ref)
    for h in range(2):
        out_ref[:, h * HALF : (h + 1) * HALF] = halves[h].astype(BF)


def _params():
    return pltpu.CompilerParams(vmem_limit_bytes=VMEM)


def _cost(flops, moved):
    return pl.CostEstimate(flops=int(flops), bytes_accessed=int(moved), transcendentals=0)


def _shape(shape, dtype):
    return jax.ShapeDtypeStruct(shape, dtype)


def _hbm(value):
    return pltpu.with_memory_space_constraint(value, pltpu.HBM)


def _fixed(*shape):
    return pl.BlockSpec(shape, lambda i, c: (0,) * len(shape))


def _half_pass(kernel, other, weights, state, out, scratch, flops, moved, name, aliases={}):
    def group(i, c):
        return 2 * i + (1 - c[0] if other else c[0])

    block = {
        "row": pl.BlockSpec((COLS, HID), lambda i, c: (group(i, c), 0)),
        "column": pl.BlockSpec((HID, COLS), lambda i, c: (0, group(i, c))),
        "received": pl.BlockSpec((1, MAIN, WIDE), lambda i, c: (i, 0, 0)),
        "slots": pl.BlockSpec((ROWS, COLS), lambda i, c: (0, group(i, c))),
        "whole": pl.BlockSpec(memory_space=pl.ANY),
        "hidden": _fixed(ROWS, HID),
        "both": _fixed(ROWS, 2 * HID),
    }
    return pl.pallas_call(
        kernel,
        grid_spec=pltpu.PrefetchScalarGridSpec(
            num_scalar_prefetch=1,
            grid=(2,),
            in_specs=[block["received"]] + [block[k] for k in weights + state],
            out_specs=[block[k] for k, _ in out],
            scratch_shapes=scratch,
        ),
        out_shape=[t for _, t in out],
        input_output_aliases=aliases,
        compiler_params=_params(),
        cost_estimate=_cost(flops, moved),
        name=name,
    )


def _forward_own(core, own, w_gate, w_up):
    return _half_pass(
        _forward_own_kernel,
        False,
        ["row", "row"],
        [],
        [("slots", pltpu.HBM((ROWS, D), BF)), ("hidden", _shape((ROWS, HID), F32)), ("hidden", _shape((ROWS, HID), F32))],
        [],
        EARLY * 2 * ROWS * D * HID,
        EARLY * 9e6,
        "forward_own",
    )(core, _hbm(own), _hbm(w_gate), _hbm(w_up))


def _forward_other(core, other, w_gate, w_up, gate, up, x):
    return _half_pass(
        _forward_other_kernel,
        True,
        ["row", "row"],
        ["hidden", "hidden", "whole"],
        [
            ("slots", pltpu.HBM((ROWS, D), BF)),
            ("hidden", _shape((ROWS, HID), F32)),
            ("hidden", _shape((ROWS, HID), F32)),
            ("hidden", _shape((ROWS, HID), BF)),
        ],
        [],
        LATE * 2 * ROWS * D * HID,
        LATE * 9e6,
        "forward_other",
        {6: 0},
    )(core, other, _hbm(w_gate), _hbm(w_up), gate, up, _hbm(x))


def _backward_own(core, own, w_down):
    return _half_pass(
        _backward_own_kernel,
        False,
        ["column"],
        [],
        [("slots", pltpu.HBM((ROWS, D), BF)), ("hidden", _shape((ROWS, HID), F32))],
        [],
        EARLY * 2 * ROWS * D * HID,
        EARLY * 9e6,
        "backward_own",
    )(core, _hbm(own), _hbm(w_down))


def _backward_other(core, other, w_down, partial, gate, up, e):
    return _half_pass(
        _backward_other_kernel,
        True,
        ["column"],
        ["hidden", "hidden", "hidden", "whole"],
        [("slots", pltpu.HBM((ROWS, D), BF)), ("both", _shape((ROWS, 2 * HID), BF))],
        [pltpu.VMEM((ROWS, HID), F32)],
        LATE * ROWS * D * HID,
        LATE * 6e6,
        "backward_other",
        {6: 0},
    )(core, other, _hbm(w_down), partial, gate, up, _hbm(e))


def _result(core, hidden, hidden_p, w_down, w_down_p):
    weight = pl.BlockSpec((HID, COLS), lambda i, c: (0, 2 * i + c[0]))
    return pl.pallas_call(
        _result_kernel,
        grid_spec=pltpu.PrefetchScalarGridSpec(
            num_scalar_prefetch=1,
            grid=(2,),
            in_specs=[_fixed(ROWS, HID), _fixed(ROWS, HID), weight, weight],
            out_specs=pl.BlockSpec((1, MAIN, WIDE), lambda i, c: (i, 0, 0)),
        ),
        out_shape=pltpu.HBM((2, MAIN, WIDE), BF),
        compiler_params=_params(),
        cost_estimate=_cost(LATE * 2 * ROWS * D * HID, LATE * 7e6),
        name="result",
    )(core, hidden, hidden_p, _hbm(w_down), _hbm(w_down_p))


def _back(core, grads, grads_p, w_gate, w_up, w_gate_p, w_up_p):
    weight = pl.BlockSpec((COLS, HID), lambda i, c: (2 * i + c[0], 0))
    return pl.pallas_call(
        _back_kernel,
        grid_spec=pltpu.PrefetchScalarGridSpec(
            num_scalar_prefetch=1,
            grid=(2,),
            in_specs=[_fixed(ROWS, 2 * HID), _fixed(ROWS, 2 * HID), weight, weight, weight, weight],
            out_specs=pl.BlockSpec((1, MAIN, WIDE), lambda i, c: (i, 0, 0)),
        ),
        out_shape=pltpu.HBM((2, MAIN, WIDE), BF),
        compiler_params=_params(),
        cost_estimate=_cost(LATE * 4 * ROWS * D * HID, LATE * 11e6),
        name="back",
    )(core, grads, grads_p, _hbm(w_gate), _hbm(w_up), _hbm(w_gate_p), _hbm(w_up_p))


def _grad_in(x, grads):
    block = pl.BlockSpec((COLS, HID), lambda i: (i, 0))
    return pl.pallas_call(
        _grad_in_kernel,
        grid=(4,),
        in_specs=[pl.BlockSpec((ROWS, COLS), lambda i: (0, i)), pl.BlockSpec((ROWS, 2 * HID), lambda i: (0, 0))],
        out_specs=[block, block],
        out_shape=[_shape((D, HID), BF), _shape((D, HID), BF)],
        compiler_params=_params(),
        cost_estimate=_cost(4 * ROWS * D * HID, 13e6),
        name="grad_in",
    )(_hbm(x), grads)


def _local(kernel, out_shape, flops, moved, name, *args):
    return pl.pallas_call(
        kernel, out_shape=out_shape, compiler_params=_params(), cost_estimate=_cost(flops, moved), name=name
    )(*args)


def _exchange(packed):
    chunks = packed.reshape(2 * EXPERTS, 8, WIDE)
    got = lax.all_to_all(chunks, ("yhi", "expert"), split_axis=0, concat_axis=0, tiled=True)
    return got.reshape(2, MAIN, WIDE)


def _swap(value, axis="core"):
    return lax.ppermute(value, axis, [(0, 1), (1, 0)])


def body(tokens, cotangent, expert_ids, route_probs, w_gate, w_up, w_down):
    core = lax.axis_index("core").astype(jnp.int32).reshape(1)
    wg, wu, wd = w_gate[0], w_up[0], w_down[0]
    ids_t, probs_t = expert_ids.T, route_probs.T

    send_x = _local(_pack_rows_kernel, pltpu.HBM((2, MAIN, WIDE), BF), 2e8, 3e6, "pack_rows", _hbm(ids_t), _hbm(tokens))
    recv_x = _exchange(send_x)
    send_e, pick, weight = _local(
        _pack_grads_kernel,
        [pltpu.HBM((2, MAIN, WIDE), BF), _shape((2 * MAIN, BLOCK), BF), _shape((2 * MAIN, BLOCK), F32)],
        2e8,
        3e6,
        "pack_grads",
        _hbm(ids_t),
        _hbm(probs_t),
        _hbm(cotangent),
    )
    wd_p, wg_p, wu_p = _swap(wd), _swap(wg), _swap(wu)
    recv_x, send_e = lax.optimization_barrier((recv_x, send_e))
    recv_e = _exchange(send_e)

    x, gate, up = _forward_own(core, recv_x, wg, wu)
    x, gate, up, hidden = _forward_other(core, _swap(recv_x), wg, wu, gate, up, x)
    send_o = _result(core, hidden, _swap(hidden), wd, wd_p)
    recv_e, send_o = lax.optimization_barrier((recv_e, send_o))
    recv_o = _exchange(send_o)

    e, partial = _backward_own(core, recv_e, wd)
    e, grads = _backward_other(core, _swap(recv_e), wd, partial, gate, up, e)
    send_b = _back(core, grads, _swap(grads), wg, wu, wg_p, wu_p)
    recv_b = _exchange(send_b)

    g_gate, g_up = _grad_in(x, grads)
    hidden, e, g_gate, g_up = lax.optimization_barrier((hidden, e, g_gate, g_up))
    g_down = _dot_tn(hidden, e).astype(BF)

    mixed, inner = _local(
        _mixed_kernel,
        [_shape((BLOCK, COLS), BF), _shape((TOPK, BLOCK), F32)],
        4e8,
        3e6,
        "mixed",
        _hbm(ids_t),
        _hbm(pick),
        _hbm(weight),
        _hbm(cotangent),
        _hbm(recv_o),
    )
    inner = inner + _swap(inner)
    far = _swap(inner, "yhi")
    recv_b, g_gate, g_up, g_down = lax.optimization_barrier((recv_b, g_gate, g_up, g_down))
    grad_tokens, grad_probs = _local(
        _grad_tokens_kernel,
        [_shape((BLOCK, COLS), BF), _shape((TOPK, BLOCK), F32)],
        2e8,
        3e6,
        "grad_tokens",
        pick,
        recv_b,
        inner,
        far,
    )
    return mixed, grad_tokens, grad_probs.T, g_gate[None], g_up[None], g_down[None]


def solution(mesh):
    fine = Mesh(mesh.devices.reshape(EXPERTS, 2, 2), ("expert", "yhi", "core"))
    dp = ("yhi", "core")
    return jax.shard_map(
        body,
        mesh=fine,
        in_specs=(
            P("expert", dp),
            P("expert", dp),
            P("expert", None),
            P("expert", None),
            P("expert", None, dp),
            P("expert", None, dp),
            P("expert", dp, None),
        ),
        out_specs=(
            P("expert", dp),
            P("expert", dp),
            P("expert", None),
            P("expert", None, dp),
            P("expert", None, dp),
            P("expert", dp, None),
        ),
        check_vma=False,
    )
```
